32 devices in a mesh: clip: 4 (over x, core), tok: 8 (over z, y).
Axes of the slice: x: 2, y: 2, z: 4, core: 2. Of those that a mesh axis runs over, the one named last changes fastest.
Arguments:
- tokens: bfloat16 [16384, 1024], P(('clip', 'tok')), may hold values from -80 to 80
- slot_keys: bfloat16 [1024, 512], replicated, may hold values from -64 to 64
- w_in: bfloat16 [8, 1024, 4096], P('tok', None, 'clip'), may hold values from -0.1875 to 0.1875
- w_back: bfloat16 [8, 4096, 1024], P('tok', 'clip'), may hold values from -0.09375 to 0.09375
- w_proj: bfloat16 [1024, 512], replicated, may hold values from -0.1875 to 0.1875
- dec_source: int32 [4, 2048], P('clip'), may hold values from 0 to 4096, as said below
- mask_token: bfloat16 [512], replicated, may hold values from -80 to 80
- w_qkv: bfloat16 [512, 1536], replicated, may hold values from -8 to 8
- w_out: bfloat16 [512, 512], replicated, may hold values from -9 to 9
Outputs:
- decoded: bfloat16 [8192, 512], P(('clip', 'tok'))
The draws below stay inside these ranges and needn't reach their ends.
Inputs may be any that keep to these rules, and one draw needn't show every extreme that they name: `dec_source`: within a clip no visible index appears twice. For each aligned block of 256 decoder positions and each aligned block of 512 visible tokens, at most 32 positions of the first show tokens of the second, and some pair of blocks reaches 32 in every clip.
All inputs are finite; a program needn't handle non-finite values.
Results may differ from the reference program's by a relative error of at most 0.025.
Values may be sent and summed in bfloat16 or wider, within the bound.
No kernel may reach another device: no remote copies, remote signals or barrier semaphores. Data moves between devices by JAX's collectives and lax.ppermute only.
A program may use at most 64 MiB of HBM per device.

```python
import math
import jax
import jax.numpy as jnp
from jax import lax

D = 1024
HID = 4096
SLOTS_E = 64
DD = 512
HEADS = 16
VIS_DEV = 512
EXPERTS = 8
SLOTS = 512
HD = 32
CLIPS = 4
VIS = 4096
DEC_DEV = 256
DEC = 2048
CAP = 32


def draw_tokens(key, part):
    base = jax.random.normal(jax.random.fold_in(key, 1), (CLIPS * VIS, D), jnp.float32)
    return base.astype(jnp.bfloat16)


def draw_slot_keys(key, part):
    return (jax.random.normal(jax.random.fold_in(key, 21), (D, SLOTS), jnp.float32) * (2.5 / math.sqrt(D))).astype(jnp.bfloat16)


def draw_mask_token(key, part):
    noise = jax.random.normal(jax.random.fold_in(key, 31), (DD,), jnp.float32)
    return noise.astype(jnp.bfloat16)


def draw_w_qkv(key, part):
    base = jax.random.normal(jax.random.fold_in(key, 41), (DD, 3 * DD), jnp.float32) / math.sqrt(DD)
    return base.astype(jnp.bfloat16)


def draw_dec_source(key, part):
    groups = DEC // DEC_DEV

    def one_clip(clip_key):
        salts = [jax.random.fold_in(clip_key, index) for index in range(6)]
        levels = jax.random.randint(salts[0], (groups,), 0, 4)
        ceiling = jnp.maximum(CAP // 2 ** levels, 1)
        counts = ceiling[None, :] - jax.random.randint(salts[1], (groups, groups), 0, ceiling[None, :] // 2 + 1)
        pick_src = jax.random.randint(salts[2], (), 0, groups)
        pick_dst = jax.random.randint(salts[3], (), 0, groups)
        counts = counts.at[pick_src, pick_dst].set(CAP)
        src_orders = jax.vmap(lambda sub: jax.random.permutation(sub, VIS_DEV))(jax.random.split(salts[4], groups))
        dst_orders = jax.vmap(lambda sub: jax.random.permutation(sub, DEC_DEV))(jax.random.split(salts[5], groups))
        src_offsets = jnp.cumsum(counts, axis=1) - counts
        dst_offsets = jnp.cumsum(counts, axis=0) - counts
        dst_ends = dst_offsets + counts
        totals = jnp.sum(counts, axis=0)
        slot_index = jnp.arange(DEC_DEV).astype(jnp.int32)
        sender = jnp.sum((dst_ends[:, :, None] <= slot_index[None, None, :]).astype(jnp.int32), axis=0)
        sender = jnp.minimum(sender, groups - 1)
        column = jnp.arange(groups).astype(jnp.int32)[:, None]
        offset_in = slot_index[None, :] - dst_offsets[sender, column]
        position_in = jnp.clip(src_offsets[sender, column] + offset_in, 0, VIS_DEV - 1)
        local_row = src_orders[sender, position_in]
        source = sender * VIS_DEV + local_row
        valid = slot_index[None, :] < totals[:, None]
        chosen = jnp.where(valid, source, VIS).astype(jnp.int32)
        where_to = column * DEC_DEV + dst_orders
        filled = jnp.full((DEC,), VIS, jnp.int32)
        return filled.at[where_to.reshape(-1)].set(chosen.reshape(-1))
    return jax.vmap(one_clip)(jax.random.split(key, CLIPS))


def block_levels(key, dims, shards, smallest, top_value):
    gain, own = 1.0, jax.random.fold_in(key, 6)
    for position, parts in shards:
        steps = jnp.exp(jax.random.uniform(jax.random.fold_in(own, position), (parts,), jnp.float32, smallest / len(shards), top_value / len(shards)))
        gain = gain * jnp.repeat(steps, dims[position] // parts).reshape([-1 if axis == position else 1 for axis in range(len(dims))])
    return gain


def gaussian(rng, shape, scale, bound, cuts=(), held_as=jnp.bfloat16):
    array = jax.random.normal(rng, shape, jnp.float32) * scale
    if len(cuts) > 0:
        array = block_levels(rng, shape, cuts, -0.22, 0.18) * array
    return jnp.clip(array, min=-bound, max=bound).astype(held_as)


def setup_inputs(seed: int = 0) -> dict:
    splits = jax.random.split(jax.random.key(seed), 10)
    return {
        "tokens": draw_tokens(jax.random.fold_in(splits[9], 71), 0),
        "slot_keys": draw_slot_keys(jax.random.fold_in(splits[9], 71), 0),
        "w_in": gaussian(splits[2], (EXPERTS, D, HID), D ** -0.5, 0.1875, ((0, 8), (2, 4))),
        "w_back": gaussian(splits[3], (EXPERTS, HID, D), HID ** -0.5, 0.09375, ((0, 8), (1, 4))),
        "w_proj": gaussian(splits[4], (D, DD), D ** -0.5, 0.1875),
        "dec_source": draw_dec_source(jax.random.fold_in(splits[9], 71), 0),
        "mask_token": draw_mask_token(jax.random.fold_in(splits[9], 71), 0),
        "w_qkv": draw_w_qkv(jax.random.fold_in(splits[9], 71), 0),
        "w_out": gaussian(splits[8], (DD, DD), 1.5, 9.0),
    }


def layer_norm(values):
    centre = values - lax.optimization_barrier(jnp.mean(values, axis=-1, keepdims=True))
    spread = lax.optimization_barrier(jnp.mean(centre * centre, axis=-1, keepdims=True))
    return centre * lax.rsqrt(spread + 1e-05)

def sinusoid(places, width):
    half = width // 2
    speeds = jnp.exp(-math.log(10000.0) * jnp.arange(half).astype(jnp.float32) / half)
    angles = places.astype(jnp.float32)[:, None] * speeds[None, :]
    return jnp.concatenate([jnp.sin(angles), jnp.cos(angles)], axis=1)

def attend(queries, key_rows, value_rows):
    heads_here, head_dim, count = queries.shape
    block = math.gcd(count, 512)
    scale = 1.0 / math.sqrt(head_dim)
    blocks = queries.reshape(heads_here, head_dim, count // block, block).transpose(2, 0, 1, 3)

    def one_block(query_block):
        scores = jnp.einsum('hkq,hkn->hqn', query_block.astype(jnp.float32), key_rows.astype(jnp.float32)) * scale
        highest = lax.optimization_barrier(jnp.max(scores, axis=-1))
        raised = jnp.exp(scores - highest[..., None]).astype(jnp.bfloat16)
        totals = lax.optimization_barrier(jnp.sum(raised.astype(jnp.float32), axis=-1))
        summed = jnp.einsum('hqn,hkn->hkq', raised.astype(jnp.float32), value_rows.astype(jnp.float32))
        return (summed / totals[:, None, :]).astype(jnp.bfloat16)
    outcome = lax.map(one_block, blocks)
    return outcome.transpose(1, 2, 0, 3).reshape(heads_here, head_dim, count)

def reference(tokens, slot_keys, w_in, w_back, w_proj, dec_source, mask_token, w_qkv, w_out):
    clip_tokens = tokens.reshape(CLIPS, VIS, D)

    def one_clip(inputs):
        clip_rows, listing = inputs
        normed = layer_norm(clip_rows.astype(jnp.float32)).astype(jnp.bfloat16)
        logits = jnp.dot(normed.astype(jnp.float32), slot_keys.astype(jnp.float32), preferred_element_type=jnp.float32)
        col_top = lax.optimization_barrier(jnp.max(logits, axis=0))
        dispatch = jnp.exp(logits - col_top[None, :]).astype(jnp.bfloat16)
        slot_sums = jnp.dot(dispatch.T.astype(jnp.float32), normed.astype(jnp.float32), preferred_element_type=jnp.float32)
        slot_totals = lax.optimization_barrier(jnp.sum(dispatch.astype(jnp.float32), axis=0))
        slot_in = (slot_sums / slot_totals[:, None]).astype(jnp.bfloat16)

        def expert(inputs_e):
            rows_e, first, second = inputs_e
            hidden = jax.nn.gelu(jnp.dot(rows_e.astype(jnp.float32), first.astype(jnp.float32), preferred_element_type=jnp.float32)).astype(jnp.bfloat16)
            return jnp.dot(hidden.astype(jnp.float32), second.astype(jnp.float32), preferred_element_type=jnp.float32).astype(jnp.bfloat16)
        slot_out = lax.map(expert, (slot_in.reshape(EXPERTS, SLOTS_E, D), w_in, w_back)).reshape(SLOTS, D)
        row_top = lax.optimization_barrier(jnp.max(logits, axis=1, keepdims=True))
        raised = jnp.exp(logits - row_top)
        combine = (raised / lax.optimization_barrier(jnp.sum(raised, axis=1, keepdims=True))).astype(jnp.bfloat16)
        moe = jnp.dot(combine.astype(jnp.float32), slot_out.astype(jnp.float32), preferred_element_type=jnp.float32).astype(jnp.bfloat16)
        projected = jnp.dot(moe.astype(jnp.float32), w_proj.astype(jnp.float32), preferred_element_type=jnp.float32).astype(jnp.bfloat16)
        places = jnp.arange(DEC).astype(jnp.int32)
        filler = (mask_token.astype(jnp.float32)[None, :] + sinusoid(places, DD)).astype(jnp.bfloat16)
        visible = listing < VIS
        picked = jnp.take(projected, jnp.minimum(listing, VIS - 1).astype(jnp.int32), axis=0)
        dec_in = jnp.where(visible[:, None], picked, filler)
        dec_normed = layer_norm(dec_in.astype(jnp.float32)).astype(jnp.bfloat16)
        qkv = jnp.einsum('pd,dchk->chkp', dec_normed.astype(jnp.float32), w_qkv.reshape(DD, 3, HEADS, HD).astype(jnp.float32)).astype(jnp.bfloat16)
        attended = attend(qkv[0], qkv[1], qkv[2])
        mixed = jnp.einsum('hkp,hke->pe', attended.astype(jnp.float32), w_out.reshape(HEADS, HD, DD).astype(jnp.float32))
        return (mixed + dec_in.astype(jnp.float32)).astype(jnp.bfloat16)
    decoded = lax.map(one_clip, (clip_tokens, dec_source))
    return decoded.reshape(CLIPS * DEC, DD)
```

```python
import math

import jax
import jax.numpy as jnp
from jax import lax
from jax.experimental import pallas as pl
from jax.experimental.pallas import tpu as pltpu
from jax.sharding import PartitionSpec as P

HEADS = 16
LANES = 128
F32 = jnp.float32
BF16 = jnp.bfloat16


def normalise(values):
    centre = values - jnp.mean(values, axis=-1, keepdims=True)
    spread = jnp.mean(centre * centre, axis=-1, keepdims=True)
    return centre * lax.rsqrt(spread + 1e-05)


def thirds(column):
    high = column.astype(BF16)
    rest = column - high.astype(F32)
    middle = rest.astype(BF16)
    low = (rest - middle.astype(F32)).astype(BF16)
    return high, middle, low


def front_kernel(tokens_ref, keys_ref, sums_ref, combine_ref):
    rows, width = tokens_ref.shape
    slots = keys_ref.shape[1]
    normed = normalise(tokens_ref[...].astype(F32)).astype(BF16)
    logits = jnp.dot(normed, keys_ref[...], preferred_element_type=F32)
    top = jnp.max(logits, axis=0, keepdims=True)
    dispatch = jnp.exp(logits - top).astype(BF16)
    turned = dispatch.T
    sums_ref[:, :width] = jnp.dot(turned, normed, preferred_element_type=F32).astype(BF16)
    totals = jnp.dot(turned, jnp.ones((rows, LANES), BF16), preferred_element_type=F32)
    tops = jnp.broadcast_to(top, (LANES, slots)).T
    lane = lax.broadcasted_iota(jnp.int32, (slots, LANES), 1)
    packed = jnp.zeros((slots, LANES), F32)
    for place, piece in enumerate(thirds(tops) + thirds(totals)):
        packed = jnp.where(lane == place, piece.astype(F32), packed)
    sums_ref[:, width:] = packed.astype(BF16)
    raised = jnp.exp(logits - jnp.max(logits, axis=1, keepdims=True))
    combine_ref[...] = (raised / jnp.sum(raised, axis=1, keepdims=True)).astype(BF16)


def front(tokens, slot_keys):
    rows, width = tokens.shape
    slots = slot_keys.shape[1]
    return pl.pallas_call(
        front_kernel,
        out_shape=(
            jax.ShapeDtypeStruct((slots, width + LANES), BF16),
            jax.ShapeDtypeStruct((rows, slots), BF16),
        ),
        compiler_params=pltpu.CompilerParams(vmem_limit_bytes=40 << 20),
    )(tokens, slot_keys)


def tail_kernel(place_ref, combine_ref, slot_ref, filler_ref, w_qkv_ref, w_out_ref, out_ref, k_ref, v_ref, a_ref):
    mine, width = out_ref.shape
    total = combine_ref.shape[0]
    head_dim = width // HEADS
    groups = width // LANES
    in_group = LANES // head_dim
    slot_rows = slot_ref[...]
    w_kv = w_qkv_ref[:, width:]

    def positions(block):
        rows = pl.ds(pl.multiple_of(block * mine, mine), mine)
        shown = jnp.dot(combine_ref[rows, :], slot_rows, preferred_element_type=F32).astype(BF16)
        dec_in = shown.astype(F32) + filler_ref[rows, :].astype(F32)
        return rows, dec_in, normalise(dec_in).astype(BF16)

    ones = jnp.ones((mine, LANES), BF16)

    @pl.loop(0, total // mine)
    def _(block):
        rows, _, normed = positions(block)
        kv = jnp.dot(normed, w_kv, preferred_element_type=F32).astype(BF16)
        for group in range(groups):
            k_ref[group, rows, :] = kv[:, group * LANES : (group + 1) * LANES]
            v_ref[group, rows, :LANES] = kv[:, width + group * LANES : width + (group + 1) * LANES]
            v_ref[group, rows, LANES:] = ones

    _, dec_in, normed = positions(place_ref[0])
    queries = jnp.dot(normed, w_qkv_ref[:, :width], preferred_element_type=F32).astype(BF16)
    for group in range(groups):
        a_ref[group] = queries[:, group * LANES : (group + 1) * LANES]
    head_of = lax.broadcasted_iota(jnp.int32, (mine, LANES), 1) // head_dim
    factor = math.log2(math.e) / math.sqrt(head_dim)

    @pl.loop(0, groups)
    def _(group):
        q_group = a_ref[group]
        result = jnp.zeros((mine, LANES), F32)
        for head in range(in_group):
            q_head = jnp.where(head_of == head, q_group, jnp.zeros_like(q_group))
            scores = lax.dot_general(
                q_head, k_ref[group], (((1,), (1,)), ((), ())), preferred_element_type=F32
            )
            highest = jnp.max(scores, axis=1, keepdims=True)
            raised = jnp.exp2((scores - highest) * factor).astype(BF16)
            both = jnp.dot(raised, v_ref[group], preferred_element_type=F32)
            result = jnp.where(head_of == head, both[:, :LANES] / both[:, LANES:], result)
        a_ref[group] = result.astype(BF16)

    attended = jnp.concatenate([a_ref[group] for group in range(groups)], axis=1)
    mixed = jnp.dot(attended, w_out_ref[...], preferred_element_type=F32)
    out_ref[...] = (mixed + dec_in).astype(BF16)


def tail(place, combine, slot_rows, filler, w_qkv, w_out, mine):
    total, width = filler.shape
    groups = width // LANES
    vmem = pl.BlockSpec(memory_space=pltpu.VMEM)
    return pl.pallas_call(
        tail_kernel,
        out_shape=jax.ShapeDtypeStruct((mine, width), BF16),
        in_specs=[pl.BlockSpec(memory_space=pltpu.SMEM)] + [vmem] * 5,
        out_specs=vmem,
        scratch_shapes=[
            pltpu.VMEM((groups, total, LANES), BF16),
            pltpu.VMEM((groups, total, 2 * LANES), BF16),
            pltpu.VMEM((groups, mine, LANES), BF16),
        ],
        compiler_params=pltpu.CompilerParams(vmem_limit_bytes=48 << 20),
    )(place, combine, slot_rows, filler, w_qkv, w_out)


def sinusoid_table(count, block, width):
    half = width // 2
    speeds = jnp.exp(-math.log(10000.0) * jnp.arange(half).astype(F32) / half)
    far = (jnp.arange(count // block) * block).astype(F32)[:, None] * speeds[None, :]
    near = jnp.arange(block).astype(F32)[:, None] * speeds[None, :]
    far_sin, far_cos = jnp.sin(far)[:, None, :], jnp.cos(far)[:, None, :]
    near_sin, near_cos = jnp.sin(near)[None], jnp.cos(near)[None]
    sines = far_sin * near_cos + far_cos * near_sin
    cosines = far_cos * near_cos - far_sin * near_sin
    return jnp.concatenate([sines, cosines], axis=2).reshape(count, width)


def unpack(stats):
    parts = stats[..., :6].astype(F32)
    top = parts[..., 0:1] + parts[..., 1:2] + parts[..., 2:3]
    total = parts[..., 3:4] + parts[..., 4:5] + parts[..., 5:6]
    return top, total


def per_device(tokens, slot_keys, w_in, w_back, w_proj, dec_source, mask_token, w_qkv, w_out):
    vis_dev, width = tokens.shape
    n_tok = lax.axis_size("tok")
    n_clip = lax.axis_size("clip")
    slots = slot_keys.shape[1]
    slots_e = slots // n_tok
    dec_width = w_proj.shape[1]
    listing = dec_source[0]
    dec_total = listing.shape[0]
    dec_dev = dec_total // n_tok
    vis_all = vis_dev * n_tok
    myself = lax.axis_index("tok")
    capacity = dec_dev // n_tok

    blocks = listing.reshape(n_tok, dec_dev)
    owners = blocks // vis_dev
    earlier = jnp.arange(dec_dev)[:, None] > jnp.arange(dec_dev)[None, :]
    same = (owners[:, :, None] == owners[:, None, :]) & earlier[None]
    ranks = jnp.sum(same.astype(jnp.int32), axis=2)
    visible = blocks < vis_all
    places = jnp.where(visible, owners * capacity + jnp.minimum(ranks, capacity - 1), -1)
    wanted = myself * capacity + jnp.arange(capacity)
    matched = places[:, None, :] == wanted[None, :, None]
    local = blocks - myself * vis_dev + 1
    source_rows = jnp.sum(jnp.where(matched, local[:, None, :], 0), axis=2) - 1
    picker = (source_rows.reshape(-1)[:, None] == jnp.arange(vis_dev)[None, :]).astype(BF16)
    placer = (places[:, :, None] == jnp.arange(dec_dev)[None, None, :]).astype(BF16)
    filler = jnp.where(
        visible.reshape(-1)[:, None],
        0.0,
        mask_token.astype(F32)[None, :] + sinusoid_table(dec_total, dec_dev, dec_width),
    ).astype(BF16)

    partial_sums, combine = front(tokens, slot_keys)
    outgoing = jnp.dot(picker, combine, preferred_element_type=F32).astype(BF16)
    spread = lax.all_gather(outgoing, "tok", axis=0)
    arrived = lax.all_to_all(
        partial_sums.reshape(n_tok, slots_e, width + LANES), "tok", split_axis=0, concat_axis=0, tiled=True
    )
    tops, totals = unpack(arrived[..., width:])
    scales = jnp.exp(tops - jnp.max(tops, axis=0, keepdims=True))
    slot_in = (
        jnp.sum(arrived[..., :width].astype(F32) * scales, axis=0) / jnp.sum(totals * scales, axis=0)
    ).astype(BF16)
    hidden = jax.nn.gelu(
        jnp.dot(
            lax.all_gather(slot_in, "clip", axis=0, tiled=True), w_in[0], preferred_element_type=F32
        )
    ).astype(BF16)
    partial_out = jnp.dot(hidden, w_back[0], preferred_element_type=F32).astype(BF16)
    partial_proj = jnp.dot(partial_out, w_proj, preferred_element_type=F32).astype(BF16)
    pieces = lax.all_to_all(
        partial_proj.reshape(n_clip, slots_e, dec_width), "clip", split_axis=0, concat_axis=0, tiled=True
    )
    slot_proj = jnp.sum(pieces.astype(F32), axis=0).astype(BF16)
    slot_rows = lax.all_to_all(
        jnp.broadcast_to(slot_proj[None], (n_tok, slots_e, dec_width)), "tok", split_axis=0, concat_axis=0, tiled=True
    ).reshape(slots, dec_width)
    by_block = spread.reshape(n_tok, n_tok, capacity, slots).transpose(1, 0, 2, 3)
    ordered = jnp.einsum(
        "bps,bsw->bpw", placer, by_block.reshape(n_tok, dec_dev, slots), preferred_element_type=F32
    ).astype(BF16)
    return tail(
        myself.reshape(1).astype(jnp.int32), ordered.reshape(dec_total, slots), slot_rows, filler, w_qkv, w_out, dec_dev
    )


def solution(mesh):
    placed = (
        P(("clip", "tok"), None),
        P(),
        P("tok", None, "clip"),
        P("tok", "clip", None),
        P(),
        P("clip", None),
        P(),
        P(),
        P(),
    )
    return jax.shard_map(
        per_device, mesh=mesh, in_specs=placed, out_specs=P(("clip", "tok"), None), check_vma=False
    )
```

```python
import math

import jax
import jax.numpy as jnp
from jax import lax
from jax.experimental import pallas as pl
from jax.experimental.pallas import tpu as pltpu
from jax.sharding import PartitionSpec as P

HEADS = 16
LANES = 128
F32 = jnp.float32
BF16 = jnp.bfloat16
VMEM = pl.BlockSpec(memory_space=pltpu.VMEM)
SMEM = pl.BlockSpec(memory_space=pltpu.SMEM)
HBM = pl.BlockSpec(memory_space=pltpu.HBM)


def normalise(values):
    centre = values - jnp.mean(values, axis=-1, keepdims=True)
    spread = jnp.mean(centre * centre, axis=-1, keepdims=True)
    return centre * lax.rsqrt(spread + 1e-05)


def thirds(column):
    high = column.astype(BF16)
    rest = column - high.astype(F32)
    middle = rest.astype(BF16)
    low = (rest - middle.astype(F32)).astype(BF16)
    return high, middle, low


def pack(tops, totals):
    rows = max(tops.shape[0], totals.shape[0])
    lane = lax.broadcasted_iota(jnp.int32, (rows, LANES), 1)
    packed = jnp.zeros((rows, LANES), F32)
    for place, piece in enumerate(thirds(tops) + thirds(totals)):
        packed = jnp.where(lane == place, piece.astype(F32), packed)
    return packed.astype(BF16)


def unpack(stats):
    parts = stats.astype(F32)
    top = parts[:, 0:1] + parts[:, 1:2] + parts[:, 2:3]
    total = parts[:, 3:4] + parts[:, 4:5] + parts[:, 5:6]
    return top, total


def swap(values, axis, mask):
    count = lax.axis_size(axis)
    return lax.ppermute(values, axis, [(index, index ^ mask) for index in range(count)])


def bit_orders(count):
    bits = list(range(count.bit_length() - 1))
    first = bits[1:2] + bits[0:1] + bits[2:]
    second = bits
    return first, second


def ranks_of(order):
    steps = len(order)
    return [
        sum(((place >> (steps - 1 - step)) & 1) << bit for step, bit in enumerate(order))
        for place in range(1 << steps)
    ]


def gather_bits(values, axis, order):
    pieces = [values]
    for bit in order:
        held = pieces[0] if len(pieces) == 1 else jnp.concatenate(pieces, axis=0)
        pieces.append(swap(held, axis, 1 << bit))
    return pieces


def gathered_ranks(order):
    held = [0]
    for bit in order:
        held = held + [index ^ (1 << bit) for index in held]
    return held


def front_kernel(orders, place_ref, tokens_hbm, keys_hbm, *refs):
    outs, combine_ref = refs[:4], refs[4]
    tokens_ref, keys_ref, turned_ref, tops_ref, picked_ref, picked_tops_ref, sems = refs[5:]
    rows, width = tokens_ref.shape
    slots = keys_ref.shape[1]
    pieces = sems.shape[1]
    token_step, key_step = rows // pieces, width // pieces
    copies = []
    for piece in range(pieces):
        part = pl.ds(piece * token_step, token_step)
        copies.append(pltpu.make_async_copy(tokens_hbm.at[part], tokens_ref.at[part], sems.at[0, piece]))
    for piece in range(pieces):
        part = pl.ds(piece * key_step, key_step)
        copies.append(pltpu.make_async_copy(keys_hbm.at[part], keys_ref.at[part], sems.at[1, piece]))
    for copy in copies:
        copy.start()
    parts = []
    for piece in range(pieces):
        copies[piece].wait()
        part = tokens_ref[piece * token_step : (piece + 1) * token_step, :].astype(F32)
        parts.append(normalise(part).astype(BF16))
    normed = jnp.concatenate(parts, axis=0)
    for copy in copies[pieces:]:
        copy.wait()
    logits = jnp.dot(normed, keys_ref[...], preferred_element_type=F32)
    top = jnp.max(logits, axis=0, keepdims=True)
    turned_ref[...] = jnp.exp(logits - top).astype(BF16).T
    tops_ref[...] = jnp.broadcast_to(top, (LANES, slots)).T
    myself = place_ref[0]
    count = 1 << len(orders[0])
    block = slots // count
    half = block // 2
    for path, order in enumerate(orders):
        for place, relative in enumerate(ranks_of(order)):
            source = pl.ds(pl.multiple_of((myself ^ relative) * block + path * half, half), half)
            target = pl.ds((path * count + place) * half, half)
            picked_ref[target, :] = turned_ref[source, :]
            picked_tops_ref[target, :] = tops_ref[source, :]
    picked = picked_ref[...]
    sums = jnp.dot(picked, normed, preferred_element_type=F32).astype(BF16)
    totals = jnp.dot(picked, jnp.ones((rows, LANES), BF16), preferred_element_type=F32)
    stats = pack(picked_tops_ref[...], totals)
    quarter = slots // 4
    for index, out_ref in enumerate(outs):
        out_ref[:, :width] = sums[index * quarter : (index + 1) * quarter, :]
        out_ref[:, width:] = stats[index * quarter : (index + 1) * quarter, :]
    raised = jnp.exp(logits - jnp.max(logits, axis=1, keepdims=True))
    combine_ref[...] = (raised / jnp.sum(raised, axis=1, keepdims=True)).astype(BF16)


def front(place, tokens, slot_keys, orders):
    rows, width = tokens.shape
    slots = slot_keys.shape[1]
    quarter = jax.ShapeDtypeStruct((slots // 4, width + LANES), BF16)
    pieces = 4
    return pl.pallas_call(
        lambda *refs: front_kernel(orders, *refs),
        out_shape=(quarter,) * 4 + (jax.ShapeDtypeStruct((rows, slots), BF16),),
        in_specs=[SMEM, HBM, HBM],
        out_specs=(VMEM,) * 5,
        scratch_shapes=[
            pltpu.VMEM((rows, width), BF16),
            pltpu.VMEM((width, slots), BF16),
            pltpu.VMEM((slots, rows), BF16),
            pltpu.VMEM((slots, LANES), F32),
            pltpu.VMEM((slots, rows), BF16),
            pltpu.VMEM((slots, LANES), F32),
            pltpu.SemaphoreType.DMA((2, pieces)),
        ],
        compiler_params=pltpu.CompilerParams(vmem_limit_bytes=28 << 20),
    )(place, tokens, slot_keys)


def merge_kernel(kept_ref, came_ref, *outs):
    width = kept_ref.shape[1] - LANES
    kept_top, kept_total = unpack(kept_ref[:, width:])
    came_top, came_total = unpack(came_ref[:, width:])
    top = jnp.maximum(kept_top, came_top)
    kept_scale, came_scale = jnp.exp(kept_top - top), jnp.exp(came_top - top)
    total = kept_total * kept_scale + came_total * came_scale
    sums = kept_ref[:, :width].astype(F32) * kept_scale + came_ref[:, :width].astype(F32) * came_scale
    if len(outs) == 1:
        outs[0][...] = (sums / total).astype(BF16)
        return
    sums = sums.astype(BF16)
    stats = pack(top, total)
    half = kept_ref.shape[0] // 2
    for index, out_ref in enumerate(outs):
        out_ref[:, :width] = sums[index * half : (index + 1) * half, :]
        out_ref[:, width:] = stats[index * half : (index + 1) * half, :]


def merge(kept, came, last):
    rows, columns = kept.shape
    if last:
        shape, specs = jax.ShapeDtypeStruct((rows, columns - LANES), BF16), VMEM
    else:
        shape, specs = (jax.ShapeDtypeStruct((rows // 2, columns), BF16),) * 2, (VMEM, VMEM)
    return pl.pallas_call(
        merge_kernel,
        out_shape=shape,
        in_specs=[VMEM, VMEM],
        out_specs=specs,
        compiler_params=pltpu.CompilerParams(vmem_limit_bytes=12 << 20),
    )(kept, came)


def experts_kernel(count, *refs):
    rows_refs, (in_a, in_b, back_a, back_b, proj_ref), outs = refs[:count], refs[count : count + 5], refs[count + 5 :]
    rows = jnp.concatenate([ref[...] for ref in rows_refs], axis=0)
    total = None
    for first_ref, second_ref in ((in_a, back_a), (in_b, back_b)):
        hidden = jax.nn.gelu(jnp.dot(rows, first_ref[...], preferred_element_type=F32)).astype(BF16)
        part = jnp.dot(hidden, second_ref[...], preferred_element_type=F32)
        total = part if total is None else total + part
    result = jnp.dot(total.astype(BF16), proj_ref[...], preferred_element_type=F32).astype(BF16)
    step = rows_refs[0].shape[0]
    for index, out_ref in enumerate(outs):
        out_ref[...] = result[index * step : (index + 1) * step, :]


def experts(slot_rows, first, first_other, second, second_other, w_proj):
    count = len(slot_rows)
    rows = slot_rows[0].shape[0]
    return pl.pallas_call(
        lambda *refs: experts_kernel(count, *refs),
        out_shape=(jax.ShapeDtypeStruct((rows, w_proj.shape[1]), BF16),) * count,
        in_specs=[VMEM] * (count + 5),
        out_specs=(VMEM,) * count,
        compiler_params=pltpu.CompilerParams(vmem_limit_bytes=24 << 20),
    )(*slot_rows, first, first_other, second, second_other, w_proj)


def order_kernel(ranks, first_count, places_ref, *refs):
    pieces, out_ref = refs[:-1], refs[-1]
    halves = (pieces[:first_count], pieces[first_count:])
    total, slots = out_ref.shape
    count = len(ranks[0])
    block = total // count
    capacity = block // count
    column = lax.broadcasted_iota(jnp.int32, (block, block), 1)
    for target in range(count):
        path, inner = divmod(target, count // 2)
        rows = [None] * count
        place = 0
        for ref in halves[path]:
            for index in range(ref.shape[0] // (block // 2)):
                start = index * (block // 2) + inner * capacity
                rows[ranks[path][place]] = ref[start : start + capacity, :]
                place += 1
        chosen = (places_ref[target * block : (target + 1) * block, :] == column).astype(BF16)
        out_ref[target * block : (target + 1) * block, :] = jnp.dot(
            chosen, jnp.concatenate(rows, axis=0), preferred_element_type=F32
        ).astype(BF16)


def put_in_order(places, first, second, ranks):
    total, slots = places.shape[0], first[0].shape[1]
    return pl.pallas_call(
        lambda *refs: order_kernel(ranks, len(first), *refs),
        out_shape=jax.ShapeDtypeStruct((total, slots), BF16),
        in_specs=[VMEM] * (1 + len(first) + len(second)),
        out_specs=VMEM,
        compiler_params=pltpu.CompilerParams(vmem_limit_bytes=24 << 20),
    )(places, *first, *second)


def tail_kernel(
    ranks, first_count, place_ref, combine_ref, filler_ref, w_qkv_ref, w_out_ref, *refs
):
    pieces = refs[:-5]
    out_ref, slot_ref, k_ref, v_ref, a_ref = refs[-5:]
    mine, width = out_ref.shape
    total = combine_ref.shape[0]
    head_dim = width // HEADS
    groups = width // LANES
    in_group = LANES // head_dim
    myself = place_ref[0]
    half = pieces[0].shape[0]
    for path, refs_here in enumerate((pieces[:first_count], pieces[first_count:])):
        place = 0
        for ref in refs_here:
            for index in range(ref.shape[0] // half):
                target = pl.multiple_of((myself ^ ranks[path][place]) * (2 * half) + path * half, half)
                slot_ref[pl.ds(target, half), :] = ref[index * half : (index + 1) * half, :]
                place += 1
    slot_rows = slot_ref[...]
    w_kv = w_qkv_ref[:, width:]

    def positions(block):
        rows = pl.ds(pl.multiple_of(block * mine, mine), mine)
        shown = jnp.dot(combine_ref[rows, :], slot_rows, preferred_element_type=F32).astype(BF16)
        dec_in = shown.astype(F32) + filler_ref[rows, :].astype(F32)
        return rows, dec_in, normalise(dec_in).astype(BF16)

    ones = jnp.ones((mine, LANES), BF16)

    @pl.loop(0, total // mine)
    def _(block):
        rows, _, normed = positions(block)
        kv = jnp.dot(normed, w_kv, preferred_element_type=F32).astype(BF16)
        for group in range(groups):
            k_ref[group, rows, :] = kv[:, group * LANES : (group + 1) * LANES]
            v_ref[group, rows, :LANES] = kv[:, width + group * LANES : width + (group + 1) * LANES]
            v_ref[group, rows, LANES:] = ones

    _, dec_in, normed = positions(myself)
    queries = jnp.dot(normed, w_qkv_ref[:, :width], preferred_element_type=F32).astype(BF16)
    for group in range(groups):
        a_ref[group] = queries[:, group * LANES : (group + 1) * LANES]
    head_of = lax.broadcasted_iota(jnp.int32, (mine, LANES), 1) // head_dim
    factor = math.log2(math.e) / math.sqrt(head_dim)

    @pl.loop(0, groups)
    def _(group):
        q_group = a_ref[group]
        result = jnp.zeros((mine, LANES), F32)
        for head in range(in_group):
            q_head = jnp.where(head_of == head, q_group, jnp.zeros_like(q_group))
            scores = lax.dot_general(
                q_head, k_ref[group], (((1,), (1,)), ((), ())), preferred_element_type=F32
            )
            highest = jnp.max(scores, axis=1, keepdims=True)
            raised = jnp.exp2((scores - highest) * factor).astype(BF16)
            both = jnp.dot(raised, v_ref[group], preferred_element_type=F32)
            result = jnp.where(head_of == head, both[:, :LANES] / both[:, LANES:], result)
        a_ref[group] = result.astype(BF16)

    attended = jnp.concatenate([a_ref[group] for group in range(groups)], axis=1)
    mixed = jnp.dot(attended, w_out_ref[...], preferred_element_type=F32)
    out_ref[...] = (mixed + dec_in).astype(BF16)


def tail(place, combine, filler, w_qkv, w_out, first, second, ranks):
    total, width = filler.shape
    groups = width // LANES
    mine = total // len(ranks[0])
    return pl.pallas_call(
        lambda *refs: tail_kernel(ranks, len(first), *refs),
        out_shape=jax.ShapeDtypeStruct((mine, width), BF16),
        in_specs=[SMEM] + [VMEM] * (4 + len(first) + len(second)),
        out_specs=VMEM,
        scratch_shapes=[
            pltpu.VMEM((combine.shape[1], width), BF16),
            pltpu.VMEM((groups, total, LANES), BF16),
            pltpu.VMEM((groups, total, 2 * LANES), BF16),
            pltpu.VMEM((groups, mine, LANES), BF16),
        ],
        compiler_params=pltpu.CompilerParams(vmem_limit_bytes=36 << 20),
    )(place, combine, filler, w_qkv, w_out, *first, *second)


def sinusoid_table(count, block, width):
    half = width // 2
    speeds = jnp.exp(-math.log(10000.0) * jnp.arange(half).astype(F32) / half)
    far = (jnp.arange(count // block) * block).astype(F32)[:, None] * speeds[None, :]
    near = jnp.arange(block).astype(F32)[:, None] * speeds[None, :]
    far_sin, far_cos = jnp.sin(far)[:, None, :], jnp.cos(far)[:, None, :]
    near_sin, near_cos = jnp.sin(near)[None], jnp.cos(near)[None]
    sines = far_sin * near_cos + far_cos * near_sin
    cosines = far_cos * near_cos - far_sin * near_sin
    return jnp.concatenate([sines, cosines], axis=2).reshape(count, width)


def per_device(tokens, slot_keys, w_in, w_back, w_proj, dec_source, mask_token, w_qkv, w_out):
    vis_dev, width = tokens.shape
    n_tok = lax.axis_size("tok")
    n_clip = lax.axis_size("clip")
    slots = slot_keys.shape[1]
    dec_width = w_proj.shape[1]
    listing = dec_source[0]
    dec_total = listing.shape[0]
    dec_dev = dec_total // n_tok
    vis_all = vis_dev * n_tok
    myself = lax.axis_index("tok").astype(jnp.int32)
    capacity = dec_dev // n_tok
    orders = bit_orders(n_tok)
    back_orders = tuple(order[::-1] for order in orders)
    ranks = tuple(gathered_ranks(order) for order in back_orders)

    blocks = listing.reshape(n_tok, dec_dev)
    owners = blocks // vis_dev
    earlier = jnp.arange(dec_dev)[:, None] > jnp.arange(dec_dev)[None, :]
    same = (owners[:, :, None] == owners[:, None, :]) & earlier[None]
    order_here = jnp.minimum(jnp.sum(same.astype(jnp.int32), axis=2), capacity - 1)
    visible = blocks < vis_all
    matched = (owners[:, None, :] == myself) & (order_here[:, None, :] == jnp.arange(capacity)[None, :, None])
    local = blocks - myself * vis_dev + 1
    source_rows = jnp.sum(jnp.where(matched, local[:, None, :], 0), axis=2) - 1
    picker = (source_rows.reshape(-1)[:, None] == jnp.arange(vis_dev)[None, :]).astype(BF16)
    places = jnp.where(visible, (owners ^ myself) * capacity + order_here, -1).reshape(dec_total, 1)
    filler = jnp.where(
        visible.reshape(-1)[:, None],
        0.0,
        mask_token.astype(F32)[None, :] + sinusoid_table(dec_total, dec_dev, dec_width),
    ).astype(BF16)

    first, first_other = w_in[0], swap(w_in[0], "clip", 1)
    second, second_other = w_back[0], swap(w_back[0], "clip", 1)

    *quarters, combine = front(myself.reshape(1), tokens, slot_keys, orders)
    state = [(quarters[0], quarters[1]), (quarters[2], quarters[3])]
    for step in range(len(orders[0])):
        last = step == len(orders[0]) - 1
        arrived = [swap(state[path][1], "tok", 1 << orders[path][step]) for path in range(2)]
        state = [merge(state[path][0], arrived[path], last) for path in range(2)]
    slot_in = jnp.concatenate(state, axis=0)

    outgoing = jnp.dot(picker, combine, preferred_element_type=F32).astype(BF16)
    cut = outgoing.shape[0] // 2
    spread = [
        gather_bits(outgoing[path * cut : (path + 1) * cut], "tok", back_orders[path]) for path in range(2)
    ]
    ordered = put_in_order(places, spread[0], spread[1], ranks)

    others = [2 * step for step in range(1, n_clip // 2)]
    rows = [slot_in] + [swap(slot_in, "clip", mask) for mask in others]
    results = experts(rows, first, first_other, second, second_other, w_proj)
    slot_proj = results[0].astype(F32)
    for mask, result in zip(others, results[1:]):
        slot_proj = slot_proj + swap(result, "clip", mask).astype(F32)
    slot_proj = slot_proj.astype(BF16)
    cut = slot_proj.shape[0] // 2
    everyone = [
        gather_bits(slot_proj[path * cut : (path + 1) * cut], "tok", back_orders[path]) for path in range(2)
    ]
    return tail(myself.reshape(1), ordered, filler, w_qkv, w_out, everyone[0], everyone[1], ranks)


def solution(mesh):
    placed = (
        P(("clip", "tok"), None),
        P(),
        P("tok", None, "clip"),
        P("tok", "clip", None),
        P(),
        P("clip", None),
        P(),
        P(),
        P(),
    )
    return jax.shard_map(
        per_device, mesh=mesh, in_specs=placed, out_specs=P(("clip", "tok"), None), check_vma=False
    )
```

```python
import math

import jax
import jax.numpy as jnp
from jax import lax
from jax.experimental import pallas as pl
from jax.experimental.pallas import tpu as pltpu
from jax.sharding import PartitionSpec as P

HEADS = 16
LANES = 128
F32 = jnp.float32
BF16 = jnp.bfloat16
VMEM = pl.BlockSpec(memory_space=pltpu.VMEM)
SMEM = pl.BlockSpec(memory_space=pltpu.SMEM)
HBM = pl.BlockSpec(memory_space=pltpu.HBM)


def normalise(values):
    centre = values - jnp.mean(values, axis=-1, keepdims=True)
    spread = jnp.mean(centre * centre, axis=-1, keepdims=True)
    return centre * lax.rsqrt(spread + 1e-05)


def thirds(column):
    high = column.astype(BF16)
    rest = column - high.astype(F32)
    middle = rest.astype(BF16)
    low = (rest - middle.astype(F32)).astype(BF16)
    return high, middle, low


def pack(tops, totals):
    rows = max(tops.shape[0], totals.shape[0])
    lane = lax.broadcasted_iota(jnp.int32, (rows, LANES), 1)
    packed = jnp.zeros((rows, LANES), F32)
    for place, piece in enumerate(thirds(tops) + thirds(totals)):
        packed = jnp.where(lane == place, piece.astype(F32), packed)
    return packed.astype(BF16)


def unpack(stats):
    parts = stats.astype(F32)
    top = parts[:, 0:1] + parts[:, 1:2] + parts[:, 2:3]
    total = parts[:, 3:4] + parts[:, 4:5] + parts[:, 5:6]
    return top, total


def swap(values, axis, mask):
    count = lax.axis_size(axis)
    return lax.ppermute(values, axis, [(index, index ^ mask) for index in range(count)])


def bit_orders(count):
    bits = list(range(count.bit_length() - 1))
    first = bits[1:2] + bits[0:1] + bits[2:]
    second = bits
    return first, second


def ranks_of(order):
    steps = len(order)
    return [
        sum(((place >> (steps - 1 - step)) & 1) << bit for step, bit in enumerate(order))
        for place in range(1 << steps)
    ]


def gather_pair(values, axis, orders):
    rows = values.shape[0]
    half = rows // 2
    arrays, steps = [values], []
    starts = [[(0, 0)], [(0, half)]]
    for step, (first, second) in enumerate(zip(*orders)):
        together = orders[0][: step + 1] == orders[1][: step + 1]
        if together:
            held = arrays[0] if len(arrays) == 1 else jnp.concatenate(arrays, axis=0)
            count = held.shape[0] // rows
            arrays.append(swap(held, axis, 1 << first))
            for path in range(2):
                starts[path] = starts[path] + [(len(arrays) - 1, index * rows + path * half) for index in range(count)]
            steps.append([arrays[-1]])
            continue
        fresh = []
        for path, bit in enumerate((first, second)):
            held = jnp.concatenate([arrays[index][row : row + half] for index, row in starts[path]], axis=0)
            fresh.append(swap(held, axis, 1 << bit))
        for path in range(2):
            index = len(arrays) + path
            starts[path] = starts[path] + [(index, place * half) for place in range(len(starts[path]))]
        arrays = arrays + fresh
        steps.append(fresh)
    return arrays, starts, steps


def tie(values, others):
    kept = lax.optimization_barrier((tuple(values), tuple(others)))
    return kept[0]


def gathered_ranks(order):
    held = [0]
    for bit in order:
        held = held + [index ^ (1 << bit) for index in held]
    return held


def front_kernel(orders, place_ref, tokens_hbm, keys_hbm, *refs):
    outs, combine_ref = refs[:4], refs[4]
    tokens_ref, keys_ref, turned_ref, tops_ref, picked_ref, picked_tops_ref, sems = refs[5:]
    rows, width = tokens_ref.shape
    slots = keys_ref.shape[1]
    pieces = sems.shape[1]
    token_step, key_step = rows // pieces, width // pieces
    copies = []
    for piece in range(pieces):
        part = pl.ds(piece * token_step, token_step)
        copies.append(pltpu.make_async_copy(tokens_hbm.at[part], tokens_ref.at[part], sems.at[0, piece]))
    for piece in range(pieces):
        part = pl.ds(piece * key_step, key_step)
        copies.append(pltpu.make_async_copy(keys_hbm.at[part], keys_ref.at[part], sems.at[1, piece]))
    for copy in copies:
        copy.start()
    parts = []
    for piece in range(pieces):
        copies[piece].wait()
        part = tokens_ref[piece * token_step : (piece + 1) * token_step, :].astype(F32)
        parts.append(normalise(part).astype(BF16))
    normed = jnp.concatenate(parts, axis=0)
    for copy in copies[pieces:]:
        copy.wait()
    logits = jnp.dot(normed, keys_ref[...], preferred_element_type=F32)
    top = jnp.max(logits, axis=0, keepdims=True)
    turned_ref[...] = jnp.exp(logits - top).astype(BF16).T
    tops_ref[...] = jnp.broadcast_to(top, (LANES, slots)).T
    myself = place_ref[0]
    count = 1 << len(orders[0])
    block = slots // count
    half = block // 2
    for path, order in enumerate(orders):
        for place, relative in enumerate(ranks_of(order)):
            source = pl.ds(pl.multiple_of((myself ^ relative) * block + path * half, half), half)
            target = pl.ds((path * count + place) * half, half)
            picked_ref[target, :] = turned_ref[source, :]
            picked_tops_ref[target, :] = tops_ref[source, :]
    picked = picked_ref[...]
    sums = jnp.dot(picked, normed, preferred_element_type=F32).astype(BF16)
    totals = jnp.dot(picked, jnp.ones((rows, LANES), BF16), preferred_element_type=F32)
    stats = pack(picked_tops_ref[...], totals)
    quarter = slots // 4
    for index, out_ref in enumerate(outs):
        out_ref[:, :width] = sums[index * quarter : (index + 1) * quarter, :]
        out_ref[:, width:] = stats[index * quarter : (index + 1) * quarter, :]
    raised = jnp.exp(logits - jnp.max(logits, axis=1, keepdims=True))
    combine_ref[...] = (raised / jnp.sum(raised, axis=1, keepdims=True)).astype(BF16)


def front(place, tokens, slot_keys, orders):
    rows, width = tokens.shape
    slots = slot_keys.shape[1]
    quarter = jax.ShapeDtypeStruct((slots // 4, width + LANES), BF16)
    pieces = 4
    return pl.pallas_call(
        lambda *refs: front_kernel(orders, *refs),
        out_shape=(quarter,) * 4 + (jax.ShapeDtypeStruct((rows, slots), BF16),),
        in_specs=[SMEM, HBM, HBM],
        out_specs=(VMEM,) * 5,
        scratch_shapes=[
            pltpu.VMEM((rows, width), BF16),
            pltpu.VMEM((width, slots), BF16),
            pltpu.VMEM((slots, rows), BF16),
            pltpu.VMEM((slots, LANES), F32),
            pltpu.VMEM((slots, rows), BF16),
            pltpu.VMEM((slots, LANES), F32),
            pltpu.SemaphoreType.DMA((2, pieces)),
        ],
        compiler_params=pltpu.CompilerParams(vmem_limit_bytes=28 << 20),
    )(place, tokens, slot_keys)


def merge_kernel(kept_ref, came_ref, *outs):
    width = kept_ref.shape[1] - LANES
    kept_top, kept_total = unpack(kept_ref[:, width:])
    came_top, came_total = unpack(came_ref[:, width:])
    top = jnp.maximum(kept_top, came_top)
    kept_scale, came_scale = jnp.exp(kept_top - top), jnp.exp(came_top - top)
    total = kept_total * kept_scale + came_total * came_scale
    sums = kept_ref[:, :width].astype(F32) * kept_scale + came_ref[:, :width].astype(F32) * came_scale
    if len(outs) == 1:
        outs[0][...] = (sums / total).astype(BF16)
        return
    sums = sums.astype(BF16)
    stats = pack(top, total)
    half = kept_ref.shape[0] // 2
    for index, out_ref in enumerate(outs):
        out_ref[:, :width] = sums[index * half : (index + 1) * half, :]
        out_ref[:, width:] = stats[index * half : (index + 1) * half, :]


def merge(kept, came, last):
    rows, columns = kept.shape
    if last:
        shape, specs = jax.ShapeDtypeStruct((rows, columns - LANES), BF16), VMEM
    else:
        shape, specs = (jax.ShapeDtypeStruct((rows // 2, columns), BF16),) * 2, (VMEM, VMEM)
    return pl.pallas_call(
        merge_kernel,
        out_shape=shape,
        in_specs=[VMEM, VMEM],
        out_specs=specs,
        compiler_params=pltpu.CompilerParams(vmem_limit_bytes=12 << 20),
    )(kept, came)


def experts_kernel(count, *refs):
    rows_refs, (in_a, in_b, back_a, back_b, proj_ref), outs = refs[:count], refs[count : count + 5], refs[count + 5 :]
    rows = jnp.concatenate([ref[...] for ref in rows_refs], axis=0)
    total = None
    for first_ref, second_ref in ((in_a, back_a), (in_b, back_b)):
        hidden = jax.nn.gelu(jnp.dot(rows, first_ref[...], preferred_element_type=F32)).astype(BF16)
        part = jnp.dot(hidden, second_ref[...], preferred_element_type=F32)
        total = part if total is None else total + part
    result = jnp.dot(total.astype(BF16), proj_ref[...], preferred_element_type=F32).astype(BF16)
    step = rows_refs[0].shape[0]
    for index, out_ref in enumerate(outs):
        out_ref[...] = result[index * step : (index + 1) * step, :]


def experts(slot_rows, first, first_other, second, second_other, w_proj):
    count = len(slot_rows)
    rows = slot_rows[0].shape[0]
    return pl.pallas_call(
        lambda *refs: experts_kernel(count, *refs),
        out_shape=(jax.ShapeDtypeStruct((rows, w_proj.shape[1]), BF16),) * count,
        in_specs=[VMEM] * (count + 5),
        out_specs=(VMEM,) * count,
        compiler_params=pltpu.CompilerParams(vmem_limit_bytes=16 << 20),
    )(*slot_rows, first, first_other, second, second_other, w_proj)


def slots_of(listing, vis_dev, count, capacity):
    block = listing.shape[1]
    owners = listing // vis_dev
    across = jnp.broadcast_to(owners, (block, block))
    before = lax.broadcasted_iota(jnp.int32, (block, block), 0) < lax.broadcasted_iota(jnp.int32, (block, block), 1)
    same = (across == across.T) & before
    ranks = jnp.sum(same.astype(F32), axis=0, keepdims=True).astype(jnp.int32)
    return owners, jnp.minimum(ranks, capacity - 1)


def pick_kernel(count, place_ref, listing_ref, combine_ref, out_ref):
    vis_dev = combine_ref.shape[0]
    block = listing_ref.shape[1] // count
    capacity = block // count
    myself = place_ref[0]
    row = lax.broadcasted_iota(jnp.int32, (capacity, block), 0)
    token = lax.broadcasted_iota(jnp.int32, (capacity, vis_dev), 1)
    picks = []
    for target in range(count):
        listing = listing_ref[:, target * block : (target + 1) * block]
        owners, ranks = slots_of(listing, vis_dev, count, capacity)
        mine = jnp.where(owners == myself, ranks, -1)
        local = jnp.broadcast_to(listing - myself * vis_dev + 1, (capacity, block))
        source = jnp.sum(jnp.where(mine == row, local, 0).astype(F32), axis=1, keepdims=True).astype(jnp.int32) - 1
        picks.append((source == token).astype(BF16))
    picker = jnp.concatenate(picks, axis=0)
    out_ref[...] = jnp.dot(picker, combine_ref[...], preferred_element_type=F32).astype(BF16)


def pick(place, listing, combine, count):
    return pl.pallas_call(
        lambda *refs: pick_kernel(count, *refs),
        out_shape=jax.ShapeDtypeStruct((listing.shape[1] // count, combine.shape[1]), BF16),
        in_specs=[SMEM, VMEM, VMEM],
        out_specs=VMEM,
        compiler_params=pltpu.CompilerParams(vmem_limit_bytes=12 << 20),
    )(place, listing, combine)


def order_kernel(ranks, starts, vis_dev, place_ref, listing_ref, filler_ref, *refs):
    pieces, out_ref, masked_ref = refs[:-2], refs[-2], refs[-1]
    total, slots = out_ref.shape
    count = len(ranks[0])
    block = total // count
    capacity = block // count
    myself = place_ref[0]
    slot = lax.broadcasted_iota(jnp.int32, (block, block), 0)
    for target in range(count):
        path, inner = divmod(target, count // 2)
        rows = [None] * count
        for relative, (index, start) in zip(ranks[path], starts[path]):
            first = start + inner * capacity
            rows[relative] = pieces[index][first : first + capacity, :]
        listing = listing_ref[:, target * block : (target + 1) * block]
        owners, order = slots_of(listing, vis_dev, count, capacity)
        visible = listing < count * vis_dev
        places = jnp.where(visible, (owners ^ myself) * capacity + order, -1)
        chosen = (places == slot).astype(F32).T.astype(BF16)
        here = pl.ds(target * block, block)
        out_ref[here, :] = jnp.dot(chosen, jnp.concatenate(rows, axis=0), preferred_element_type=F32).astype(BF16)
        shown = jnp.broadcast_to(visible.astype(F32), (LANES, block)).T[:, 0:1]
        masked_ref[here, :] = jnp.where(shown > 0.5, jnp.zeros((), F32), filler_ref[here, :].astype(F32)).astype(BF16)


def put_in_order(place, listing, filler, arrays, starts, ranks, vis_dev):
    total, width = filler.shape
    slots = arrays[0].shape[1]
    return pl.pallas_call(
        lambda *refs: order_kernel(ranks, starts, vis_dev, *refs),
        out_shape=(jax.ShapeDtypeStruct((total, slots), BF16), jax.ShapeDtypeStruct((total, width), BF16)),
        in_specs=[SMEM] + [VMEM] * (2 + len(arrays)),
        out_specs=(VMEM, VMEM),
        compiler_params=pltpu.CompilerParams(vmem_limit_bytes=20 << 20),
    )(place, listing, filler, *arrays)


def tail_kernel(
    ranks, starts, place_ref, combine_ref, filler_ref, w_qkv_ref, w_out_ref, *refs
):
    pieces = refs[:-5]
    out_ref, slot_ref, k_ref, v_ref, a_ref = refs[-5:]
    mine, width = out_ref.shape
    total = combine_ref.shape[0]
    head_dim = width // HEADS
    groups = width // LANES
    in_group = LANES // head_dim
    myself = place_ref[0]
    half = pieces[0].shape[0] // 2
    for path in range(2):
        for relative, (index, start) in zip(ranks[path], starts[path]):
            target = pl.multiple_of((myself ^ relative) * (2 * half) + path * half, half)
            slot_ref[pl.ds(target, half), :] = pieces[index][start : start + half, :]
    slot_rows = slot_ref[...]
    w_kv = w_qkv_ref[:, width:]

    def positions(block, many=1):
        rows = pl.ds(block * mine * many, mine * many) if isinstance(block, int) else pl.ds(pl.multiple_of(block * mine, mine), mine)
        shown = jnp.dot(combine_ref[rows, :], slot_rows, preferred_element_type=F32).astype(BF16)
        dec_in = shown.astype(F32) + filler_ref[rows, :].astype(F32)
        return rows, dec_in, normalise(dec_in).astype(BF16)

    v_ref[:, :, LANES:] = jnp.ones((groups, total, LANES), BF16)
    for block in range(total // mine // 8):
        rows, _, normed = positions(block, 8)
        kv = jnp.dot(normed, w_kv, preferred_element_type=F32).astype(BF16)
        for group in range(groups):
            k_ref[group, rows, :] = kv[:, group * LANES : (group + 1) * LANES]
            v_ref[group, rows, :LANES] = kv[:, width + group * LANES : width + (group + 1) * LANES]

    _, dec_in, normed = positions(myself)
    queries = jnp.dot(normed, w_qkv_ref[:, :width], preferred_element_type=F32).astype(BF16)
    head_of = lax.broadcasted_iota(jnp.int32, (mine, LANES), 1) // head_dim
    factor = math.log2(math.e) / math.sqrt(head_dim)

    for group in range(groups):
        q_group = queries[:, group * LANES : (group + 1) * LANES]
        result = jnp.zeros((mine, LANES), F32)
        for head in range(in_group):
            q_head = jnp.where(head_of == head, q_group, jnp.zeros_like(q_group))
            scores = lax.dot_general(
                q_head, k_ref[group], (((1,), (1,)), ((), ())), preferred_element_type=F32
            )
            highest = jnp.max(scores, axis=1, keepdims=True)
            raised = jnp.exp2((scores - highest) * factor).astype(BF16)
            both = jnp.dot(raised, v_ref[group], preferred_element_type=F32)
            result = jnp.where(head_of == head, both[:, :LANES] / both[:, LANES:], result)
        a_ref[group] = result.astype(BF16)

    attended = jnp.concatenate([a_ref[group] for group in range(groups)], axis=1)
    mixed = jnp.dot(attended, w_out_ref[...], preferred_element_type=F32)
    out_ref[...] = (mixed + dec_in).astype(BF16)


def tail(place, combine, filler, w_qkv, w_out, arrays, starts, ranks):
    total, width = filler.shape
    groups = width // LANES
    mine = total // len(ranks[0])
    return pl.pallas_call(
        lambda *refs: tail_kernel(ranks, starts, *refs),
        out_shape=jax.ShapeDtypeStruct((mine, width), BF16),
        in_specs=[SMEM] + [VMEM] * (4 + len(arrays)),
        out_specs=VMEM,
        scratch_shapes=[
            pltpu.VMEM((combine.shape[1], width), BF16),
            pltpu.VMEM((groups, total, LANES), BF16),
            pltpu.VMEM((groups, total, 2 * LANES), BF16),
            pltpu.VMEM((groups, mine, LANES), BF16),
        ],
        compiler_params=pltpu.CompilerParams(vmem_limit_bytes=32 << 20),
    )(place, combine, filler, w_qkv, w_out, *arrays)


def sinusoid_table(count, block, width):
    half = width // 2
    speeds = jnp.exp(-math.log(10000.0) * jnp.arange(half).astype(F32) / half)
    far = (jnp.arange(count // block) * block).astype(F32)[:, None] * speeds[None, :]
    near = jnp.arange(block).astype(F32)[:, None] * speeds[None, :]
    far_sin, far_cos = jnp.sin(far)[:, None, :], jnp.cos(far)[:, None, :]
    near_sin, near_cos = jnp.sin(near)[None], jnp.cos(near)[None]
    sines = far_sin * near_cos + far_cos * near_sin
    cosines = far_cos * near_cos - far_sin * near_sin
    return jnp.concatenate([sines, cosines], axis=2).reshape(count, width)


def per_device(tokens, slot_keys, w_in, w_back, w_proj, dec_source, mask_token, w_qkv, w_out):
    vis_dev, width = tokens.shape
    n_tok = lax.axis_size("tok")
    n_clip = lax.axis_size("clip")
    slots = slot_keys.shape[1]
    dec_width = w_proj.shape[1]
    dec_total = dec_source.shape[1]
    dec_dev = dec_total // n_tok
    myself = lax.axis_index("tok").astype(jnp.int32)
    place = myself.reshape(1)
    orders = bit_orders(n_tok)
    back_orders = tuple(order[::-1] for order in orders)
    ranks = tuple(gathered_ranks(order) for order in back_orders)
    steps = len(orders[0])

    first, first_other = w_in[0], swap(w_in[0], "clip", 1)
    second, second_other = w_back[0], swap(w_back[0], "clip", 1)

    *quarters, combine = front(place, tokens, slot_keys, orders)

    outgoing = pick(place, dec_source, combine, n_tok)
    arrays, starts, brought = gather_pair(outgoing, "tok", back_orders)
    (late_mask,) = tie([mask_token], [quarters[1]])
    filler = (late_mask.astype(F32)[None, :] + sinusoid_table(dec_total, dec_dev, dec_width)).astype(BF16)
    ordered, filler = put_in_order(place, dec_source, filler, arrays, starts, ranks, vis_dev)

    state = [(quarters[0], quarters[1]), (quarters[2], quarters[3])]
    for step in range(steps):
        last = step == steps - 1
        sent = [state[path][1] for path in range(2)]
        if last:
            sent = tie(sent, brought[0])
        arrived = [swap(sent[path], "tok", 1 << orders[path][step]) for path in range(2)]
        state = [merge(state[path][0], arrived[path], last) for path in range(2)]
    slot_in = jnp.concatenate(state, axis=0)

    (slot_in,) = tie([slot_in], [array for group in brought[1:-1] for array in group])
    others = [2 * step for step in range(1, n_clip // 2)]
    rows = [slot_in] + [swap(slot_in, "clip", mask) for mask in others]
    results = experts(rows, first, first_other, second, second_other, w_proj)
    slot_proj = results[0].astype(F32)
    for mask, result in zip(others, results[1:]):
        slot_proj = slot_proj + swap(result, "clip", mask).astype(F32)
    (slot_proj,) = tie([slot_proj.astype(BF16)], brought[-1])
    everyone, their_starts, _ = gather_pair(slot_proj, "tok", back_orders)
    return tail(place, ordered, filler, w_qkv, w_out, everyone, their_starts, ranks)


def solution(mesh):
    placed = (
        P(("clip", "tok"), None),
        P(),
        P("tok", None, "clip"),
        P("tok", "clip", None),
        P(),
        P("clip", None),
        P(),
        P(),
        P(),
    )
    return jax.shard_map(
        per_device, mesh=mesh, in_specs=placed, out_specs=P(("clip", "tok"), None), check_vma=False
    )
```

```python
import math

import jax
import jax.numpy as jnp
from jax import lax
from jax.experimental import pallas as pl
from jax.experimental.pallas import tpu as pltpu
from jax.sharding import PartitionSpec as P

HEADS = 16
LANES = 128
F32 = jnp.float32
BF16 = jnp.bfloat16
VMEM = pl.BlockSpec(memory_space=pltpu.VMEM)
SMEM = pl.BlockSpec(memory_space=pltpu.SMEM)
HBM = pl.BlockSpec(memory_space=pltpu.HBM)


def normalise(values):
    centre = values - jnp.mean(values, axis=-1, keepdims=True)
    spread = jnp.mean(centre * centre, axis=-1, keepdims=True)
    return centre * lax.rsqrt(spread + 1e-05)


def thirds(column):
    high = column.astype(BF16)
    rest = column - high.astype(F32)
    middle = rest.astype(BF16)
    low = (rest - middle.astype(F32)).astype(BF16)
    return high, middle, low


def pack(tops, totals):
    rows = max(tops.shape[0], totals.shape[0])
    lane = lax.broadcasted_iota(jnp.int32, (rows, LANES), 1)
    packed = jnp.zeros((rows, LANES), F32)
    for place, piece in enumerate(thirds(tops) + thirds(totals)):
        packed = jnp.where(lane == place, piece.astype(F32), packed)
    return packed.astype(BF16)


def unpack(stats):
    parts = stats.astype(F32)
    top = parts[:, 0:1] + parts[:, 1:2] + parts[:, 2:3]
    total = parts[:, 3:4] + parts[:, 4:5] + parts[:, 5:6]
    return top, total


def swap(values, axis, mask):
    count = lax.axis_size(axis)
    return lax.ppermute(values, axis, [(index, index ^ mask) for index in range(count)])


def bit_orders(count):
    bits = list(range(count.bit_length() - 1))
    first = bits[1:2] + bits[0:1] + bits[2:]
    second = bits
    return first, second


def ranks_of(order):
    steps = len(order)
    return [
        sum(((place >> (steps - 1 - step)) & 1) << bit for step, bit in enumerate(order))
        for place in range(1 << steps)
    ]


def gather_pair(values, axis, orders):
    rows = values.shape[0]
    half = rows // 2
    arrays, steps = [values], []
    starts = [[(0, 0)], [(0, half)]]
    for step, (first, second) in enumerate(zip(*orders)):
        together = orders[0][: step + 1] == orders[1][: step + 1]
        if together:
            held = arrays[0] if len(arrays) == 1 else jnp.concatenate(arrays, axis=0)
            count = held.shape[0] // rows
            arrays.append(swap(held, axis, 1 << first))
            for path in range(2):
                starts[path] = starts[path] + [(len(arrays) - 1, index * rows + path * half) for index in range(count)]
            steps.append([arrays[-1]])
            continue
        fresh = []
        for path, bit in enumerate((first, second)):
            held = jnp.concatenate([arrays[index][row : row + half] for index, row in starts[path]], axis=0)
            fresh.append(swap(held, axis, 1 << bit))
        for path in range(2):
            index = len(arrays) + path
            starts[path] = starts[path] + [(index, place * half) for place in range(len(starts[path]))]
        arrays = arrays + fresh
        steps.append(fresh)
    return arrays, starts, steps


def tie(values, others):
    kept = lax.optimization_barrier((tuple(values), tuple(others)))
    return kept[0]


def gathered_ranks(order):
    held = [0]
    for bit in order:
        held = held + [index ^ (1 << bit) for index in held]
    return held


def front_kernel(orders, place_ref, tokens_hbm, keys_hbm, *refs):
    outs, combine_ref = refs[:4], refs[4]
    tokens_ref, keys_ref, turned_ref, tops_ref, picked_ref, picked_tops_ref, sems = refs[5:]
    rows, width = tokens_ref.shape
    slots = keys_ref.shape[1]
    pieces = sems.shape[1]
    token_step, key_step = rows // pieces, width // pieces
    copies = []
    for piece in range(pieces):
        part = pl.ds(piece * token_step, token_step)
        copies.append(pltpu.make_async_copy(tokens_hbm.at[part], tokens_ref.at[part], sems.at[0, piece]))
    for piece in range(pieces):
        part = pl.ds(piece * key_step, key_step)
        copies.append(pltpu.make_async_copy(keys_hbm.at[part], keys_ref.at[part], sems.at[1, piece]))
    for copy in copies:
        copy.start()
    parts = []
    for piece in range(pieces):
        copies[piece].wait()
        part = tokens_ref[piece * token_step : (piece + 1) * token_step, :].astype(F32)
        parts.append(normalise(part).astype(BF16))
    normed = jnp.concatenate(parts, axis=0)
    for copy in copies[pieces:]:
        copy.wait()
    logits = jnp.dot(normed, keys_ref[...], preferred_element_type=F32)
    top = jnp.max(logits, axis=0, keepdims=True)
    turned_ref[...] = jnp.exp(logits - top).astype(BF16).T
    tops_ref[...] = jnp.broadcast_to(top, (LANES, slots)).T
    myself = place_ref[0]
    count = 1 << len(orders[0])
    block = slots // count
    half = block // 2
    for path, order in enumerate(orders):
        for place, relative in enumerate(ranks_of(order)):
            source = pl.ds(pl.multiple_of((myself ^ relative) * block + path * half, half), half)
            target = pl.ds((path * count + place) * half, half)
            picked_ref[target, :] = turned_ref[source, :]
            picked_tops_ref[target, :] = tops_ref[source, :]
    picked = picked_ref[...]
    sums = jnp.dot(picked, normed, preferred_element_type=F32).astype(BF16)
    totals = jnp.dot(picked, jnp.ones((rows, LANES), BF16), preferred_element_type=F32)
    stats = pack(picked_tops_ref[...], totals)
    quarter = slots // 4
    for index, out_ref in enumerate(outs):
        out_ref[:, :width] = sums[index * quarter : (index + 1) * quarter, :]
        out_ref[:, width:] = stats[index * quarter : (index + 1) * quarter, :]
    raised = jnp.exp(logits - jnp.max(logits, axis=1, keepdims=True))
    combine_ref[...] = (raised / jnp.sum(raised, axis=1, keepdims=True)).astype(BF16)


def front(place, tokens, slot_keys, orders):
    rows, width = tokens.shape
    slots = slot_keys.shape[1]
    quarter = jax.ShapeDtypeStruct((slots // 4, width + LANES), BF16)
    pieces = 4
    return pl.pallas_call(
        lambda *refs: front_kernel(orders, *refs),
        out_shape=(quarter,) * 4 + (jax.ShapeDtypeStruct((rows, slots), BF16),),
        in_specs=[SMEM, HBM, HBM],
        out_specs=(VMEM,) * 5,
        scratch_shapes=[
            pltpu.VMEM((rows, width), BF16),
            pltpu.VMEM((width, slots), BF16),
            pltpu.VMEM((slots, rows), BF16),
            pltpu.VMEM((slots, LANES), F32),
            pltpu.VMEM((slots, rows), BF16),
            pltpu.VMEM((slots, LANES), F32),
            pltpu.SemaphoreType.DMA((2, pieces)),
        ],
        compiler_params=pltpu.CompilerParams(vmem_limit_bytes=28 << 20),
    )(place, *(pltpu.with_memory_space_constraint(array, pltpu.HBM) for array in (tokens, slot_keys)))


def merge_kernel(kept_ref, came_ref, *outs):
    width = kept_ref.shape[1] - LANES
    kept_top, kept_total = unpack(kept_ref[:, width:])
    came_top, came_total = unpack(came_ref[:, width:])
    top = jnp.maximum(kept_top, came_top)
    kept_scale, came_scale = jnp.exp(kept_top - top), jnp.exp(came_top - top)
    total = kept_total * kept_scale + came_total * came_scale
    sums = kept_ref[:, :width].astype(F32) * kept_scale + came_ref[:, :width].astype(F32) * came_scale
    if len(outs) == 1:
        outs[0][...] = (sums / total).astype(BF16)
        return
    sums = sums.astype(BF16)
    stats = pack(top, total)
    half = kept_ref.shape[0] // 2
    for index, out_ref in enumerate(outs):
        out_ref[:, :width] = sums[index * half : (index + 1) * half, :]
        out_ref[:, width:] = stats[index * half : (index + 1) * half, :]


def merge(kept, came, last):
    rows, columns = kept.shape
    if last:
        shape, specs = jax.ShapeDtypeStruct((rows, columns - LANES), BF16), VMEM
    else:
        shape, specs = (jax.ShapeDtypeStruct((rows // 2, columns), BF16),) * 2, (VMEM, VMEM)
    return pl.pallas_call(
        merge_kernel,
        out_shape=shape,
        in_specs=[VMEM, VMEM],
        out_specs=specs,
        compiler_params=pltpu.CompilerParams(vmem_limit_bytes=12 << 20),
    )(kept, came)


def experts_kernel(count, *refs):
    rows_refs, (in_a, in_b, back_a, back_b, proj_ref), refs = refs[:count], refs[count : count + 5], refs[count + 5 :]
    outs, (in_ref, back_ref, sems) = refs[:count], refs[count:]
    copies = [
        pltpu.make_async_copy(source, target, sems.at[index])
        for index, (source, target) in enumerate(((in_b, in_ref), (back_b, back_ref)))
    ]
    for copy in copies:
        copy.start()
    rows = jnp.concatenate([ref[...] for ref in rows_refs], axis=0)

    def hidden(weights):
        return jax.nn.gelu(jnp.dot(rows, weights, preferred_element_type=F32)).astype(BF16)

    total = jnp.dot(hidden(in_a[...]), back_a[...], preferred_element_type=F32)
    copies[0].wait()
    other = hidden(in_ref[...])
    copies[1].wait()
    total = total + jnp.dot(other, back_ref[...], preferred_element_type=F32)
    result = jnp.dot(total.astype(BF16), proj_ref[...], preferred_element_type=F32).astype(BF16)
    step = rows_refs[0].shape[0]
    for index, out_ref in enumerate(outs):
        out_ref[...] = result[index * step : (index + 1) * step, :]


def experts(slot_rows, first, first_other, second, second_other, w_proj):
    count = len(slot_rows)
    rows = slot_rows[0].shape[0]
    return pl.pallas_call(
        lambda *refs: experts_kernel(count, *refs),
        out_shape=(jax.ShapeDtypeStruct((rows, w_proj.shape[1]), BF16),) * count,
        in_specs=[VMEM] * count + [VMEM, HBM, VMEM, HBM, VMEM],
        out_specs=(VMEM,) * count,
        scratch_shapes=[
            pltpu.VMEM(first.shape, BF16),
            pltpu.VMEM(second.shape, BF16),
            pltpu.SemaphoreType.DMA((2,)),
        ],
        compiler_params=pltpu.CompilerParams(vmem_limit_bytes=20 << 20),
    )(*slot_rows, first, first_other, second, second_other, w_proj)


def slots_of(listing, vis_dev, count, capacity):
    block = listing.shape[1]
    owners = listing // vis_dev
    across = jnp.broadcast_to(owners, (block, block))
    before = lax.broadcasted_iota(jnp.int32, (block, block), 0) < lax.broadcasted_iota(jnp.int32, (block, block), 1)
    same = (across == across.T) & before
    ranks = jnp.sum(same.astype(F32), axis=0, keepdims=True).astype(jnp.int32)
    return owners, jnp.minimum(ranks, capacity - 1)


def pick_kernel(count, place_ref, listing_ref, combine_ref, out_ref):
    vis_dev = combine_ref.shape[0]
    block = listing_ref.shape[1] // count
    capacity = block // count
    myself = place_ref[0]
    row = lax.broadcasted_iota(jnp.int32, (capacity, block), 0)
    token = lax.broadcasted_iota(jnp.int32, (capacity, vis_dev), 1)
    picks = []
    for target in range(count):
        listing = listing_ref[:, target * block : (target + 1) * block]
        owners, ranks = slots_of(listing, vis_dev, count, capacity)
        mine = jnp.where(owners == myself, ranks, -1)
        local = jnp.broadcast_to(listing - myself * vis_dev + 1, (capacity, block))
        source = jnp.sum(jnp.where(mine == row, local, 0).astype(F32), axis=1, keepdims=True).astype(jnp.int32) - 1
        picks.append((source == token).astype(BF16))
    picker = jnp.concatenate(picks, axis=0)
    out_ref[...] = jnp.dot(picker, combine_ref[...], preferred_element_type=F32).astype(BF16)


def pick(place, listing, combine, count):
    return pl.pallas_call(
        lambda *refs: pick_kernel(count, *refs),
        out_shape=jax.ShapeDtypeStruct((listing.shape[1] // count, combine.shape[1]), BF16),
        in_specs=[SMEM, VMEM, VMEM],
        out_specs=VMEM,
        compiler_params=pltpu.CompilerParams(vmem_limit_bytes=12 << 20),
    )(place, listing, combine)


def order_kernel(ranks, starts, vis_dev, place_ref, listing_ref, filler_ref, *refs):
    pieces, out_ref, masked_ref = refs[:-2], refs[-2], refs[-1]
    total, slots = out_ref.shape
    count = len(ranks[0])
    block = total // count
    capacity = block // count
    myself = place_ref[0]
    slot = lax.broadcasted_iota(jnp.int32, (block, block), 0)
    for target in range(count):
        path, inner = divmod(target, count // 2)
        rows = [None] * count
        for relative, (index, start) in zip(ranks[path], starts[path]):
            first = start + inner * capacity
            rows[relative] = pieces[index][first : first + capacity, :]
        listing = listing_ref[:, target * block : (target + 1) * block]
        owners, order = slots_of(listing, vis_dev, count, capacity)
        visible = listing < count * vis_dev
        places = jnp.where(visible, (owners ^ myself) * capacity + order, -1)
        chosen = (places == slot).astype(F32).T.astype(BF16)
        here = pl.ds(target * block, block)
        out_ref[here, :] = jnp.dot(chosen, jnp.concatenate(rows, axis=0), preferred_element_type=F32).astype(BF16)
        shown = jnp.broadcast_to(visible.astype(F32), (LANES, block)).T[:, 0:1]
        masked_ref[here, :] = jnp.where(shown > 0.5, jnp.zeros((), F32), filler_ref[here, :].astype(F32)).astype(BF16)


def put_in_order(place, listing, filler, arrays, starts, ranks, vis_dev):
    total, width = filler.shape
    slots = arrays[0].shape[1]
    return pl.pallas_call(
        lambda *refs: order_kernel(ranks, starts, vis_dev, *refs),
        out_shape=(jax.ShapeDtypeStruct((total, slots), BF16), jax.ShapeDtypeStruct((total, width), BF16)),
        in_specs=[SMEM] + [VMEM] * (2 + len(arrays)),
        out_specs=(VMEM, VMEM),
        compiler_params=pltpu.CompilerParams(vmem_limit_bytes=20 << 20),
    )(place, listing, filler, *arrays)


def tail_kernel(
    ranks, starts, place_ref, combine_ref, filler_ref, w_qkv_ref, w_out_ref, *refs
):
    pieces = refs[:-5]
    out_ref, slot_ref, k_ref, v_ref, a_ref = refs[-5:]
    mine, width = out_ref.shape
    total = combine_ref.shape[0]
    head_dim = width // HEADS
    groups = width // LANES
    in_group = LANES // head_dim
    myself = place_ref[0]
    half = pieces[0].shape[0] // 2
    for path in range(2):
        for relative, (index, start) in zip(ranks[path], starts[path]):
            target = pl.multiple_of((myself ^ relative) * (2 * half) + path * half, half)
            slot_ref[pl.ds(target, half), :] = pieces[index][start : start + half, :]
    slot_rows = slot_ref[...]
    w_kv = w_qkv_ref[:, width:]

    def positions(block, many=1):
        rows = pl.ds(block * mine * many, mine * many) if isinstance(block, int) else pl.ds(pl.multiple_of(block * mine, mine), mine)
        shown = jnp.dot(combine_ref[rows, :], slot_rows, preferred_element_type=F32).astype(BF16)
        dec_in = shown.astype(F32) + filler_ref[rows, :].astype(F32)
        return rows, dec_in, normalise(dec_in).astype(BF16)

    v_ref[:, :, LANES:] = jnp.ones((groups, total, LANES), BF16)
    for block in range(total // mine // 8):
        rows, _, normed = positions(block, 8)
        kv = jnp.dot(normed, w_kv, preferred_element_type=F32).astype(BF16)
        for group in range(groups):
            k_ref[group, rows, :] = kv[:, group * LANES : (group + 1) * LANES]
            v_ref[group, rows, :LANES] = kv[:, width + group * LANES : width + (group + 1) * LANES]

    _, dec_in, normed = positions(myself)
    queries = jnp.dot(normed, w_qkv_ref[:, :width], preferred_element_type=F32).astype(BF16)
    head_of = lax.broadcasted_iota(jnp.int32, (mine, LANES), 1) // head_dim
    factor = math.log2(math.e) / math.sqrt(head_dim)

    for group in range(groups):
        q_group = queries[:, group * LANES : (group + 1) * LANES]
        result = jnp.zeros((mine, LANES), F32)
        for head in range(in_group):
            q_head = jnp.where(head_of == head, q_group, jnp.zeros_like(q_group))
            scores = lax.dot_general(
                q_head, k_ref[group], (((1,), (1,)), ((), ())), preferred_element_type=F32
            )
            highest = jnp.max(scores, axis=1, keepdims=True)
            raised = jnp.exp2((scores - highest) * factor).astype(BF16)
            both = jnp.dot(raised, v_ref[group], preferred_element_type=F32)
            result = jnp.where(head_of == head, both[:, :LANES] / both[:, LANES:], result)
        a_ref[group] = result.astype(BF16)

    attended = jnp.concatenate([a_ref[group] for group in range(groups)], axis=1)
    mixed = jnp.dot(attended, w_out_ref[...], preferred_element_type=F32)
    out_ref[...] = (mixed + dec_in).astype(BF16)


def tail(place, combine, filler, w_qkv, w_out, arrays, starts, ranks):
    total, width = filler.shape
    groups = width // LANES
    mine = total // len(ranks[0])
    return pl.pallas_call(
        lambda *refs: tail_kernel(ranks, starts, *refs),
        out_shape=jax.ShapeDtypeStruct((mine, width), BF16),
        in_specs=[SMEM] + [VMEM] * (4 + len(arrays)),
        out_specs=VMEM,
        scratch_shapes=[
            pltpu.VMEM((combine.shape[1], width), BF16),
            pltpu.VMEM((groups, total, LANES), BF16),
            pltpu.VMEM((groups, total, 2 * LANES), BF16),
            pltpu.VMEM((groups, mine, LANES), BF16),
        ],
        compiler_params=pltpu.CompilerParams(vmem_limit_bytes=32 << 20),
    )(place, combine, filler, w_qkv, w_out, *arrays)


def sinusoid_table(count, block, width):
    half = width // 2
    speeds = jnp.exp(-math.log(10000.0) * jnp.arange(half).astype(F32) / half)
    far = (jnp.arange(count // block) * block).astype(F32)[:, None] * speeds[None, :]
    near = jnp.arange(block).astype(F32)[:, None] * speeds[None, :]
    far_sin, far_cos = jnp.sin(far)[:, None, :], jnp.cos(far)[:, None, :]
    near_sin, near_cos = jnp.sin(near)[None], jnp.cos(near)[None]
    sines = far_sin * near_cos + far_cos * near_sin
    cosines = far_cos * near_cos - far_sin * near_sin
    return jnp.concatenate([sines, cosines], axis=2).reshape(count, width)


def per_device(tokens, slot_keys, w_in, w_back, w_proj, dec_source, mask_token, w_qkv, w_out):
    vis_dev, width = tokens.shape
    n_tok = lax.axis_size("tok")
    n_clip = lax.axis_size("clip")
    slots = slot_keys.shape[1]
    dec_width = w_proj.shape[1]
    dec_total = dec_source.shape[1]
    dec_dev = dec_total // n_tok
    myself = lax.axis_index("tok").astype(jnp.int32)
    place = myself.reshape(1)
    orders = bit_orders(n_tok)
    back_orders = tuple(order[::-1] for order in orders)
    ranks = tuple(gathered_ranks(order) for order in back_orders)
    steps = len(orders[0])

    first, first_other = w_in[0], swap(w_in[0], "clip", 1)
    second, second_other = w_back[0], swap(w_back[0], "clip", 1)

    *quarters, combine = front(place, tokens, slot_keys, orders)

    outgoing = pick(place, dec_source, combine, n_tok)
    arrays, starts, brought = gather_pair(outgoing, "tok", back_orders)
    filler = (mask_token.astype(F32)[None, :] + sinusoid_table(dec_total, dec_dev, dec_width)).astype(BF16)
    ordered, filler = put_in_order(place, dec_source, filler, arrays, starts, ranks, vis_dev)

    state = [(quarters[0], quarters[1]), (quarters[2], quarters[3])]
    for step in range(steps):
        sent = [state[path][1] for path in range(2)]
        if step == 1:
            sent = tie(sent, brought[0])
        arrived = [swap(sent[path], "tok", 1 << orders[path][step]) for path in range(2)]
        state = [merge(state[path][0], arrived[path], step == steps - 1) for path in range(2)]
    slot_in = jnp.concatenate(state, axis=0)

    (slot_in,) = tie([slot_in], [array for group in brought[1:-1] for array in group])
    others = [2 * step for step in range(1, n_clip // 2)]
    rows = [slot_in] + [swap(slot_in, "clip", mask) for mask in others]
    results = experts(rows, first, first_other, second, second_other, w_proj)
    slot_proj = results[0].astype(F32)
    for mask, result in zip(others, results[1:]):
        slot_proj = slot_proj + swap(result, "clip", mask).astype(F32)
    (slot_proj,) = tie([slot_proj.astype(BF16)], brought[-1])
    everyone, their_starts, _ = gather_pair(slot_proj, "tok", back_orders)
    return tail(place, ordered, filler, w_qkv, w_out, everyone, their_starts, ranks)


def solution(mesh):
    placed = (
        P(("clip", "tok"), None),
        P(),
        P("tok", None, "clip"),
        P("tok", "clip", None),
        P(),
        P("clip", None),
        P(),
        P(),
        P(),
    )
    return jax.shard_map(
        per_device, mesh=mesh, in_specs=placed, out_specs=P(("clip", "tok"), None), check_vma=False
    )
```

```python
import math

import jax
import jax.numpy as jnp
from jax import lax
from jax.experimental import pallas as pl
from jax.experimental.pallas import tpu as pltpu
from jax.sharding import PartitionSpec as P

HEADS = 16
LANES = 128
F32 = jnp.float32
BF16 = jnp.bfloat16
VMEM = pl.BlockSpec(memory_space=pltpu.VMEM)
SMEM = pl.BlockSpec(memory_space=pltpu.SMEM)
HBM = pl.BlockSpec(memory_space=pltpu.HBM)


def normalise(values):
    centre = values - jnp.mean(values, axis=-1, keepdims=True)
    spread = jnp.mean(centre * centre, axis=-1, keepdims=True)
    return centre * lax.rsqrt(spread + 1e-05)


def thirds(column):
    high = column.astype(BF16)
    rest = column - high.astype(F32)
    middle = rest.astype(BF16)
    low = (rest - middle.astype(F32)).astype(BF16)
    return high, middle, low


def pack(tops, totals):
    rows = max(tops.shape[0], totals.shape[0])
    lane = lax.broadcasted_iota(jnp.int32, (rows, LANES), 1)
    packed = jnp.zeros((rows, LANES), F32)
    for place, piece in enumerate(thirds(tops) + thirds(totals)):
        packed = jnp.where(lane == place, piece.astype(F32), packed)
    return packed.astype(BF16)


def unpack(stats):
    parts = stats.astype(F32)
    top = parts[:, 0:1] + parts[:, 1:2] + parts[:, 2:3]
    total = parts[:, 3:4] + parts[:, 4:5] + parts[:, 5:6]
    return top, total


def swap(values, axis, mask):
    count = lax.axis_size(axis)
    return lax.ppermute(values, axis, [(index, index ^ mask) for index in range(count)])


def bit_orders(count):
    bits = list(range(count.bit_length() - 1))
    first = bits[1:2] + bits[0:1] + bits[2:]
    second = bits
    return first, second


def ranks_of(order):
    steps = len(order)
    return [
        sum(((place >> (steps - 1 - step)) & 1) << bit for step, bit in enumerate(order))
        for place in range(1 << steps)
    ]


def gather_pair(values, axis, orders):
    rows = values.shape[0]
    half = rows // 2
    arrays, steps = [values], []
    starts = [[(0, 0)], [(0, half)]]
    for step, (first, second) in enumerate(zip(*orders)):
        together = orders[0][: step + 1] == orders[1][: step + 1]
        if together:
            held = arrays[0] if len(arrays) == 1 else jnp.concatenate(arrays, axis=0)
            count = held.shape[0] // rows
            arrays.append(swap(held, axis, 1 << first))
            for path in range(2):
                starts[path] = starts[path] + [(len(arrays) - 1, index * rows + path * half) for index in range(count)]
            steps.append([arrays[-1]])
            continue
        fresh = []
        for path, bit in enumerate((first, second)):
            held = jnp.concatenate([arrays[index][row : row + half] for index, row in starts[path]], axis=0)
            fresh.append(swap(held, axis, 1 << bit))
        for path in range(2):
            index = len(arrays) + path
            starts[path] = starts[path] + [(index, place * half) for place in range(len(starts[path]))]
        arrays = arrays + fresh
        steps.append(fresh)
    return arrays, starts, steps


def gather_direct(values, axis):
    count = lax.axis_size(axis)
    bits = count.bit_length() - 1
    low = 1 << (bits // 2)
    rows = values.shape[0]
    near = [values] + [swap(values, axis, step) for step in range(1, low)]
    held = jnp.concatenate(near, axis=0)
    arrays = [held] + [swap(held, axis, step * low) for step in range(1, count // low)]
    ranks = [step * low + inner for step in range(count // low) for inner in range(low)]
    starts = [
        [(step, inner * rows + half) for step in range(count // low) for inner in range(low)] for half in (0, rows // 2)
    ]
    return arrays, starts, (ranks, ranks)


def tie(values, others):
    kept = lax.optimization_barrier((tuple(values), tuple(others)))
    return kept[0]


def gathered_ranks(order):
    held = [0]
    for bit in order:
        held = held + [index ^ (1 << bit) for index in held]
    return held


def slots_of(listing, vis_dev, count, capacity):
    block = listing.shape[1]
    owners = listing // vis_dev
    across = jnp.broadcast_to(owners, (block, block))
    before = lax.broadcasted_iota(jnp.int32, (block, block), 0) < lax.broadcasted_iota(jnp.int32, (block, block), 1)
    same = (across == across.T) & before
    ranks = jnp.sum(same.astype(F32), axis=0, keepdims=True).astype(jnp.int32)
    return owners, jnp.minimum(ranks, capacity - 1)


def picker_of(myself, listing_ref, vis_dev, count):
    block = listing_ref.shape[1] // count
    capacity = block // count
    row = lax.broadcasted_iota(jnp.int32, (capacity, block), 0)
    token = lax.broadcasted_iota(jnp.int32, (capacity, vis_dev), 1)
    picks = []
    for target in range(count):
        listing = listing_ref[:, target * block : (target + 1) * block]
        owners, ranks = slots_of(listing, vis_dev, count, capacity)
        mine = jnp.where(owners == myself, ranks, -1)
        local = jnp.broadcast_to(listing - myself * vis_dev + 1, (capacity, block))
        source = jnp.sum(jnp.where(mine == row, local, 0).astype(F32), axis=1, keepdims=True).astype(jnp.int32) - 1
        picks.append((source == token).astype(BF16))
    return jnp.concatenate(picks, axis=0)


def rows_kernel(count, place_ref, listing_ref, tokens_hbm, keys_hbm, picked_ref, normed_ref, logits_ref, *refs):
    tokens_ref, keys_ref, sems = refs
    rows, width = tokens_ref.shape
    pieces = sems.shape[1]
    token_step, key_step = rows // pieces, width // pieces
    copies = []
    for piece in range(pieces):
        part = pl.ds(piece * token_step, token_step)
        copies.append(pltpu.make_async_copy(tokens_hbm.at[part], tokens_ref.at[part], sems.at[0, piece]))
    for piece in range(pieces):
        part = pl.ds(piece * key_step, key_step)
        copies.append(pltpu.make_async_copy(keys_hbm.at[part], keys_ref.at[part], sems.at[1, piece]))
    for copy in copies:
        copy.start()
    picker = picker_of(place_ref[0], listing_ref, rows, count)
    parts = []
    for piece in range(pieces):
        copies[piece].wait()
        part = tokens_ref[piece * token_step : (piece + 1) * token_step, :].astype(F32)
        parts.append(normalise(part).astype(BF16))
    normed = jnp.concatenate(parts, axis=0)
    normed_ref[...] = normed
    for copy in copies[pieces:]:
        copy.wait()
    logits = jnp.dot(normed, keys_ref[...], preferred_element_type=F32)
    logits_ref[...] = logits
    raised = jnp.exp(logits - jnp.max(logits, axis=1, keepdims=True))
    combine = (raised / jnp.sum(raised, axis=1, keepdims=True)).astype(BF16)
    picked_ref[...] = jnp.dot(picker, combine, preferred_element_type=F32).astype(BF16)


def rows_and_picks(place, listing, tokens, slot_keys, count):
    rows, width = tokens.shape
    slots = slot_keys.shape[1]
    pieces = 4
    return pl.pallas_call(
        lambda *refs: rows_kernel(count, *refs),
        out_shape=(
            jax.ShapeDtypeStruct((listing.shape[1] // count, slots), BF16),
            jax.ShapeDtypeStruct((rows, width), BF16),
            jax.ShapeDtypeStruct((rows, slots), F32),
        ),
        in_specs=[SMEM, VMEM, HBM, HBM],
        out_specs=(VMEM,) * 3,
        scratch_shapes=[
            pltpu.VMEM((rows, width), BF16),
            pltpu.VMEM((width, slots), BF16),
            pltpu.SemaphoreType.DMA((2, pieces)),
        ],
        compiler_params=pltpu.CompilerParams(vmem_limit_bytes=24 << 20),
    )(place, listing, *(pltpu.with_memory_space_constraint(array, pltpu.HBM) for array in (tokens, slot_keys)))


def sums_kernel(orders, place_ref, normed_ref, logits_ref, *refs):
    outs, (turned_ref, tops_ref, picked_ref, picked_tops_ref) = refs[:4], refs[4:]
    rows, width = normed_ref.shape
    slots = logits_ref.shape[1]
    logits = logits_ref[...]
    top = jnp.max(logits, axis=0, keepdims=True)
    turned_ref[...] = jnp.exp(logits - top).astype(BF16).T
    tops_ref[...] = jnp.broadcast_to(top, (LANES, slots)).T
    myself = place_ref[0]
    count = 1 << len(orders[0])
    block = slots // count
    half = block // 2
    for path, order in enumerate(orders):
        for place, relative in enumerate(ranks_of(order)):
            source = pl.ds(pl.multiple_of((myself ^ relative) * block + path * half, half), half)
            target = pl.ds((path * count + place) * half, half)
            picked_ref[target, :] = turned_ref[source, :]
            picked_tops_ref[target, :] = tops_ref[source, :]
    picked = picked_ref[...]
    sums = jnp.dot(picked, normed_ref[...], preferred_element_type=F32).astype(BF16)
    totals = jnp.dot(picked, jnp.ones((rows, LANES), BF16), preferred_element_type=F32)
    stats = pack(picked_tops_ref[...], totals)
    quarter = slots // 4
    for index, out_ref in enumerate(outs):
        out_ref[:, :width] = sums[index * quarter : (index + 1) * quarter, :]
        out_ref[:, width:] = stats[index * quarter : (index + 1) * quarter, :]


def own_sums(place, normed, logits, orders):
    rows, width = normed.shape
    slots = logits.shape[1]
    return pl.pallas_call(
        lambda *refs: sums_kernel(orders, *refs),
        out_shape=(jax.ShapeDtypeStruct((slots // 4, width + LANES), BF16),) * 4,
        in_specs=[SMEM, VMEM, VMEM],
        out_specs=(VMEM,) * 4,
        scratch_shapes=[
            pltpu.VMEM((slots, rows), BF16),
            pltpu.VMEM((slots, LANES), F32),
            pltpu.VMEM((slots, rows), BF16),
            pltpu.VMEM((slots, LANES), F32),
        ],
        compiler_params=pltpu.CompilerParams(vmem_limit_bytes=24 << 20),
    )(place, normed, logits)


def merge_kernel(kept_ref, came_ref, *outs):
    width = kept_ref.shape[1] - LANES
    kept_top, kept_total = unpack(kept_ref[:, width:])
    came_top, came_total = unpack(came_ref[:, width:])
    top = jnp.maximum(kept_top, came_top)
    kept_scale, came_scale = jnp.exp(kept_top - top), jnp.exp(came_top - top)
    total = kept_total * kept_scale + came_total * came_scale
    sums = kept_ref[:, :width].astype(F32) * kept_scale + came_ref[:, :width].astype(F32) * came_scale
    if len(outs) == 1:
        outs[0][...] = (sums / total).astype(BF16)
        return
    sums = sums.astype(BF16)
    stats = pack(top, total)
    half = kept_ref.shape[0] // 2
    for index, out_ref in enumerate(outs):
        out_ref[:, :width] = sums[index * half : (index + 1) * half, :]
        out_ref[:, width:] = stats[index * half : (index + 1) * half, :]


def merge(kept, came, last):
    rows, columns = kept.shape
    if last:
        shape, specs = jax.ShapeDtypeStruct((rows, columns - LANES), BF16), VMEM
    else:
        shape, specs = (jax.ShapeDtypeStruct((rows // 2, columns), BF16),) * 2, (VMEM, VMEM)
    return pl.pallas_call(
        merge_kernel,
        out_shape=shape,
        in_specs=[VMEM, VMEM],
        out_specs=specs,
        compiler_params=pltpu.CompilerParams(vmem_limit_bytes=12 << 20),
    )(kept, came)


def experts_kernel(count, *refs):
    rows_refs, (in_a, in_b, back_a, back_b, proj_ref), refs = refs[:count], refs[count : count + 5], refs[count + 5 :]
    outs, (in_ref, back_ref, sems) = refs[:count], refs[count:]
    copies = [
        pltpu.make_async_copy(source, target, sems.at[index])
        for index, (source, target) in enumerate(((in_b, in_ref), (back_b, back_ref)))
    ]
    for copy in copies:
        copy.start()
    rows = jnp.concatenate([ref[...] for ref in rows_refs], axis=0)

    def hidden(weights):
        return jax.nn.gelu(jnp.dot(rows, weights, preferred_element_type=F32)).astype(BF16)

    total = jnp.dot(hidden(in_a[...]), back_a[...], preferred_element_type=F32)
    copies[0].wait()
    other = hidden(in_ref[...])
    copies[1].wait()
    total = total + jnp.dot(other, back_ref[...], preferred_element_type=F32)
    result = jnp.dot(total.astype(BF16), proj_ref[...], preferred_element_type=F32).astype(BF16)
    step = rows_refs[0].shape[0]
    for index, out_ref in enumerate(outs):
        out_ref[...] = result[index * step : (index + 1) * step, :]


def experts(slot_rows, first, first_other, second, second_other, w_proj):
    count = len(slot_rows)
    rows = slot_rows[0].shape[0]
    return pl.pallas_call(
        lambda *refs: experts_kernel(count, *refs),
        out_shape=(jax.ShapeDtypeStruct((rows, w_proj.shape[1]), BF16),) * count,
        in_specs=[VMEM] * count + [VMEM, HBM, VMEM, HBM, VMEM],
        out_specs=(VMEM,) * count,
        scratch_shapes=[
            pltpu.VMEM(first.shape, BF16),
            pltpu.VMEM(second.shape, BF16),
            pltpu.SemaphoreType.DMA((2,)),
        ],
        compiler_params=pltpu.CompilerParams(vmem_limit_bytes=20 << 20),
    )(*slot_rows, first, first_other, second, second_other, w_proj)


def order_kernel(ranks, starts, vis_dev, place_ref, listing_ref, filler_ref, *refs):
    pieces, out_ref, masked_ref = refs[:-2], refs[-2], refs[-1]
    total, slots = out_ref.shape
    count = len(ranks[0])
    block = total // count
    capacity = block // count
    myself = place_ref[0]
    slot = lax.broadcasted_iota(jnp.int32, (block, block), 0)
    for target in range(count):
        path, inner = divmod(target, count // 2)
        rows = [None] * count
        for relative, (index, start) in zip(ranks[path], starts[path]):
            first = start + inner * capacity
            rows[relative] = pieces[index][first : first + capacity, :]
        listing = listing_ref[:, target * block : (target + 1) * block]
        owners, order = slots_of(listing, vis_dev, count, capacity)
        visible = listing < count * vis_dev
        places = jnp.where(visible, (owners ^ myself) * capacity + order, -1)
        chosen = (places == slot).astype(F32).T.astype(BF16)
        here = pl.ds(target * block, block)
        out_ref[here, :] = jnp.dot(chosen, jnp.concatenate(rows, axis=0), preferred_element_type=F32).astype(BF16)
        shown = jnp.broadcast_to(visible.astype(F32), (LANES, block)).T[:, 0:1]
        masked_ref[here, :] = jnp.where(shown > 0.5, jnp.zeros((), F32), filler_ref[here, :].astype(F32)).astype(BF16)


def put_in_order(place, listing, filler, arrays, starts, ranks, vis_dev):
    total, width = filler.shape
    slots = arrays[0].shape[1]
    return pl.pallas_call(
        lambda *refs: order_kernel(ranks, starts, vis_dev, *refs),
        out_shape=(jax.ShapeDtypeStruct((total, slots), BF16), jax.ShapeDtypeStruct((total, width), BF16)),
        in_specs=[SMEM] + [VMEM] * (2 + len(arrays)),
        out_specs=(VMEM, VMEM),
        compiler_params=pltpu.CompilerParams(vmem_limit_bytes=20 << 20),
    )(place, listing, filler, *arrays)


def tail_kernel(
    ranks, starts, half, place_ref, combine_ref, filler_ref, w_qkv_ref, w_out_ref, *refs
):
    pieces = refs[:-5]
    out_ref, slot_ref, k_ref, v_ref, a_ref = refs[-5:]
    mine, width = out_ref.shape
    total = combine_ref.shape[0]
    head_dim = width // HEADS
    groups = width // LANES
    in_group = LANES // head_dim
    myself = place_ref[0]
    for path in range(2):
        for relative, (index, start) in zip(ranks[path], starts[path]):
            target = pl.multiple_of((myself ^ relative) * (2 * half) + path * half, half)
            slot_ref[pl.ds(target, half), :] = pieces[index][start : start + half, :]
    slot_rows = slot_ref[...]
    w_kv = w_qkv_ref[:, width:]

    def positions(block, many=1):
        rows = pl.ds(block * mine * many, mine * many) if isinstance(block, int) else pl.ds(pl.multiple_of(block * mine, mine), mine)
        shown = jnp.dot(combine_ref[rows, :], slot_rows, preferred_element_type=F32).astype(BF16)
        dec_in = shown.astype(F32) + filler_ref[rows, :].astype(F32)
        return rows, dec_in, normalise(dec_in).astype(BF16)

    v_ref[:, :, LANES:] = jnp.ones((groups, total, LANES), BF16)
    for block in range(total // mine // 8):
        rows, _, normed = positions(block, 8)
        kv = jnp.dot(normed, w_kv, preferred_element_type=F32).astype(BF16)
        for group in range(groups):
            k_ref[group, rows, :] = kv[:, group * LANES : (group + 1) * LANES]
            v_ref[group, rows, :LANES] = kv[:, width + group * LANES : width + (group + 1) * LANES]

    _, dec_in, normed = positions(myself)
    queries = jnp.dot(normed, w_qkv_ref[:, :width], preferred_element_type=F32).astype(BF16)
    head_of = lax.broadcasted_iota(jnp.int32, (mine, LANES), 1) // head_dim
    factor = math.log2(math.e) / math.sqrt(head_dim)

    for group in range(groups):
        q_group = queries[:, group * LANES : (group + 1) * LANES]
        result = jnp.zeros((mine, LANES), F32)
        for head in range(in_group):
            q_head = jnp.where(head_of == head, q_group, jnp.zeros_like(q_group))
            scores = lax.dot_general(
                q_head, k_ref[group], (((1,), (1,)), ((), ())), preferred_element_type=F32
            )
            highest = jnp.max(scores, axis=1, keepdims=True)
            raised = jnp.exp2((scores - highest) * factor).astype(BF16)
            both = jnp.dot(raised, v_ref[group], preferred_element_type=F32)
            result = jnp.where(head_of == head, both[:, :LANES] / both[:, LANES:], result)
        a_ref[group] = result.astype(BF16)

    attended = jnp.concatenate([a_ref[group] for group in range(groups)], axis=1)
    mixed = jnp.dot(attended, w_out_ref[...], preferred_element_type=F32)
    out_ref[...] = (mixed + dec_in).astype(BF16)


def tail(place, combine, filler, w_qkv, w_out, arrays, starts, ranks, half):
    total, width = filler.shape
    groups = width // LANES
    mine = total // len(ranks[0])
    return pl.pallas_call(
        lambda *refs: tail_kernel(ranks, starts, half, *refs),
        out_shape=jax.ShapeDtypeStruct((mine, width), BF16),
        in_specs=[SMEM] + [VMEM] * (4 + len(arrays)),
        out_specs=VMEM,
        scratch_shapes=[
            pltpu.VMEM((combine.shape[1], width), BF16),
            pltpu.VMEM((groups, total, LANES), BF16),
            pltpu.VMEM((groups, total, 2 * LANES), BF16),
            pltpu.VMEM((groups, mine, LANES), BF16),
        ],
        compiler_params=pltpu.CompilerParams(vmem_limit_bytes=32 << 20),
    )(place, combine, filler, w_qkv, w_out, *arrays)


def sinusoid_table(count, block, width):
    half = width // 2
    speeds = jnp.exp(-math.log(10000.0) * jnp.arange(half).astype(F32) / half)
    far = (jnp.arange(count // block) * block).astype(F32)[:, None] * speeds[None, :]
    near = jnp.arange(block).astype(F32)[:, None] * speeds[None, :]
    far_sin, far_cos = jnp.sin(far)[:, None, :], jnp.cos(far)[:, None, :]
    near_sin, near_cos = jnp.sin(near)[None], jnp.cos(near)[None]
    sines = far_sin * near_cos + far_cos * near_sin
    cosines = far_cos * near_cos - far_sin * near_sin
    return jnp.concatenate([sines, cosines], axis=2).reshape(count, width)


def per_device(tokens, slot_keys, w_in, w_back, w_proj, dec_source, mask_token, w_qkv, w_out):
    vis_dev, width = tokens.shape
    n_tok = lax.axis_size("tok")
    n_clip = lax.axis_size("clip")
    slots = slot_keys.shape[1]
    dec_width = w_proj.shape[1]
    dec_total = dec_source.shape[1]
    dec_dev = dec_total // n_tok
    myself = lax.axis_index("tok").astype(jnp.int32)
    place = myself.reshape(1)
    orders = bit_orders(n_tok)
    back_orders = tuple(order[::-1] for order in orders)
    ranks = tuple(gathered_ranks(order) for order in back_orders)
    steps = len(orders[0])

    first, first_other = w_in[0], swap(w_in[0], "clip", 1)
    second, second_other = w_back[0], swap(w_back[0], "clip", 1)

    outgoing, normed, logits = rows_and_picks(place, dec_source, tokens, slot_keys, n_tok)
    arrays, starts, brought = gather_pair(outgoing, "tok", back_orders)
    filler = (mask_token.astype(F32)[None, :] + sinusoid_table(dec_total, dec_dev, dec_width)).astype(BF16)
    ordered, filler = put_in_order(place, dec_source, filler, arrays, starts, ranks, vis_dev)

    quarters = own_sums(place, normed, logits, orders)
    state = [(quarters[0], quarters[1]), (quarters[2], quarters[3])]
    for step in range(steps):
        sent = [state[path][1] for path in range(2)]
        arrived = [swap(sent[path], "tok", 1 << orders[path][step]) for path in range(2)]
        state = [merge(state[path][0], arrived[path], step == steps - 1) for path in range(2)]
    slot_in = jnp.concatenate(state, axis=0)

    (slot_in,) = tie([slot_in], [array for group in brought[1:-1] for array in group])
    others = [2 * step for step in range(1, n_clip // 2)]
    rows = [slot_in] + [swap(slot_in, "clip", mask) for mask in others]
    results = experts(rows, first, first_other, second, second_other, w_proj)
    slot_proj = results[0].astype(F32)
    for mask, result in zip(others, results[1:]):
        slot_proj = slot_proj + swap(result, "clip", mask).astype(F32)
    (slot_proj,) = tie([slot_proj.astype(BF16)], brought[-1])
    everyone, their_starts, their_ranks = gather_direct(slot_proj, "tok")
    return tail(place, ordered, filler, w_qkv, w_out, everyone, their_starts, their_ranks, slot_proj.shape[0] // 2)


def solution(mesh):
    placed = (
        P(("clip", "tok"), None),
        P(),
        P("tok", None, "clip"),
        P("tok", "clip", None),
        P(),
        P("clip", None),
        P(),
        P(),
        P(),
    )
    return jax.shard_map(
        per_device, mesh=mesh, in_specs=placed, out_specs=P(("clip", "tok"), None), check_vma=False
    )
```

```python
import math

import jax
import jax.numpy as jnp
from jax import lax
from jax.experimental import pallas as pl
from jax.experimental.pallas import tpu as pltpu
from jax.sharding import PartitionSpec as P

HEADS = 16
LANES = 128
F32 = jnp.float32
BF16 = jnp.bfloat16
VMEM = pl.BlockSpec(memory_space=pltpu.VMEM)
SMEM = pl.BlockSpec(memory_space=pltpu.SMEM)
HBM = pl.BlockSpec(memory_space=pltpu.HBM)


def normalise(values):
    centre = values - jnp.mean(values, axis=-1, keepdims=True)
    spread = jnp.mean(centre * centre, axis=-1, keepdims=True)
    return centre * lax.rsqrt(spread + 1e-05)


def thirds(column):
    high = column.astype(BF16)
    rest = column - high.astype(F32)
    middle = rest.astype(BF16)
    low = (rest - middle.astype(F32)).astype(BF16)
    return high, middle, low


def pack(tops, totals):
    rows = max(tops.shape[0], totals.shape[0])
    lane = lax.broadcasted_iota(jnp.int32, (rows, LANES), 1)
    packed = jnp.zeros((rows, LANES), F32)
    for place, piece in enumerate(thirds(tops) + thirds(totals)):
        packed = jnp.where(lane == place, piece.astype(F32), packed)
    return packed.astype(BF16)


def unpack(stats):
    parts = stats.astype(F32)
    top = parts[:, 0:1] + parts[:, 1:2] + parts[:, 2:3]
    total = parts[:, 3:4] + parts[:, 4:5] + parts[:, 5:6]
    return top, total


def swap(values, axis, mask):
    count = lax.axis_size(axis)
    return lax.ppermute(values, axis, [(index, index ^ mask) for index in range(count)])


def bit_orders(count):
    bits = list(range(count.bit_length() - 1))
    first = bits[1:2] + bits[0:1] + bits[2:]
    second = bits
    return first, second


def path_shares(block):
    return (block // 4, block - block // 4) if block % 64 == 0 else (block // 2, block // 2)


def ranks_of(order):
    steps = len(order)
    return [
        sum(((place >> (steps - 1 - step)) & 1) << bit for step, bit in enumerate(order))
        for place in range(1 << steps)
    ]


def gather_pair(values, axis, orders):
    rows = values.shape[0]
    half = rows // 2
    arrays, steps = [values], []
    starts = [[(0, 0)], [(0, half)]]
    for step, (first, second) in enumerate(zip(*orders)):
        together = orders[0][: step + 1] == orders[1][: step + 1]
        if together:
            held = arrays[0] if len(arrays) == 1 else jnp.concatenate(arrays, axis=0)
            count = held.shape[0] // rows
            arrays.append(swap(held, axis, 1 << first))
            for path in range(2):
                starts[path] = starts[path] + [(len(arrays) - 1, index * rows + path * half) for index in range(count)]
            steps.append([arrays[-1]])
            continue
        fresh = []
        for path, bit in enumerate((first, second)):
            held = jnp.concatenate([arrays[index][row : row + half] for index, row in starts[path]], axis=0)
            fresh.append(swap(held, axis, 1 << bit))
        for path in range(2):
            index = len(arrays) + path
            starts[path] = starts[path] + [(index, place * half) for place in range(len(starts[path]))]
        arrays = arrays + fresh
        steps.append(fresh)
    return arrays, starts, steps


def gather_direct(values, axis):
    count = lax.axis_size(axis)
    bits = count.bit_length() - 1
    low = 1 << (bits // 2)
    rows = values.shape[0]
    near = [values] + [swap(values, axis, step) for step in range(1, low)]
    held = jnp.concatenate(near, axis=0)
    arrays = [held] + [swap(held, axis, step * low) for step in range(1, count // low)]
    ranks = [step * low + inner for step in range(count // low) for inner in range(low)]
    starts = [
        [(step, inner * rows + half) for step in range(count // low) for inner in range(low)] for half in (0, rows // 2)
    ]
    return arrays, starts, (ranks, ranks)


def tie(values, others):
    kept = lax.optimization_barrier((tuple(values), tuple(others)))
    return kept[0]


def gathered_ranks(order):
    held = [0]
    for bit in order:
        held = held + [index ^ (1 << bit) for index in held]
    return held


def slots_of(listing, vis_dev, count, capacity):
    block = listing.shape[1]
    owners = listing // vis_dev
    across = jnp.broadcast_to(owners, (block, block))
    before = lax.broadcasted_iota(jnp.int32, (block, block), 0) < lax.broadcasted_iota(jnp.int32, (block, block), 1)
    same = (across == across.T) & before
    ranks = jnp.sum(same.astype(F32), axis=0, keepdims=True).astype(jnp.int32)
    return owners, jnp.minimum(ranks, capacity - 1)


def picker_of(myself, listing_ref, vis_dev, count):
    block = listing_ref.shape[1] // count
    capacity = block // count
    row = lax.broadcasted_iota(jnp.int32, (capacity, block), 0)
    token = lax.broadcasted_iota(jnp.int32, (capacity, vis_dev), 1)
    picks = []
    for target in range(count):
        listing = listing_ref[:, target * block : (target + 1) * block]
        owners, ranks = slots_of(listing, vis_dev, count, capacity)
        mine = jnp.where(owners == myself, ranks, -1)
        local = jnp.broadcast_to(listing - myself * vis_dev + 1, (capacity, block))
        source = jnp.sum(jnp.where(mine == row, local, 0).astype(F32), axis=1, keepdims=True).astype(jnp.int32) - 1
        picks.append((source == token).astype(BF16))
    return jnp.concatenate(picks, axis=0)


def rows_kernel(count, place_ref, listing_hbm, tokens_hbm, keys_hbm, picked_ref, normed_ref, logits_ref, *refs):
    listing_ref, tokens_ref, keys_ref, listing_sem, sems = refs
    listing_copy = pltpu.make_async_copy(listing_hbm, listing_ref, listing_sem)
    listing_copy.start()
    rows, width = tokens_ref.shape
    pieces = sems.shape[1]
    token_step, key_step = rows // pieces, width // pieces
    copies = []
    for piece in range(pieces):
        part = pl.ds(piece * token_step, token_step)
        copies.append(pltpu.make_async_copy(tokens_hbm.at[part], tokens_ref.at[part], sems.at[0, piece]))
    for piece in range(pieces):
        part = pl.ds(piece * key_step, key_step)
        copies.append(pltpu.make_async_copy(keys_hbm.at[part], keys_ref.at[part], sems.at[1, piece]))
    for copy in copies:
        copy.start()
    listing_copy.wait()
    picker = picker_of(place_ref[0], listing_ref, rows, count)
    parts = []
    for piece in range(pieces):
        copies[piece].wait()
        part = tokens_ref[piece * token_step : (piece + 1) * token_step, :].astype(F32)
        parts.append(normalise(part).astype(BF16))
    normed = jnp.concatenate(parts, axis=0)
    normed_ref[...] = normed
    for copy in copies[pieces:]:
        copy.wait()
    logits = jnp.dot(normed, keys_ref[...], preferred_element_type=F32)
    logits_ref[...] = logits
    raised = jnp.exp(logits - jnp.max(logits, axis=1, keepdims=True))
    combine = (raised / jnp.sum(raised, axis=1, keepdims=True)).astype(BF16)
    picked_ref[...] = jnp.dot(picker, combine, preferred_element_type=F32).astype(BF16)


def rows_and_picks(place, listing, tokens, slot_keys, count):
    rows, width = tokens.shape
    slots = slot_keys.shape[1]
    pieces = 4
    return pl.pallas_call(
        lambda *refs: rows_kernel(count, *refs),
        out_shape=(
            jax.ShapeDtypeStruct((listing.shape[1] // count, slots), BF16),
            jax.ShapeDtypeStruct((rows, width), BF16),
            jax.ShapeDtypeStruct((rows, slots), F32),
        ),
        in_specs=[SMEM, HBM, HBM, HBM],
        out_specs=(VMEM,) * 3,
        scratch_shapes=[
            pltpu.VMEM(listing.shape, jnp.int32),
            pltpu.VMEM((rows, width), BF16),
            pltpu.VMEM((width, slots), BF16),
            pltpu.SemaphoreType.DMA,
            pltpu.SemaphoreType.DMA((2, pieces)),
        ],
        compiler_params=pltpu.CompilerParams(vmem_limit_bytes=24 << 20),
    )(place, *(pltpu.with_memory_space_constraint(array, pltpu.HBM) for array in (listing, tokens, slot_keys)))


def sums_kernel(orders, place_ref, normed_ref, logits_ref, *refs):
    outs, (turned_ref, tops_ref, picked_ref, picked_tops_ref) = refs[:4], refs[4:]
    rows, width = normed_ref.shape
    slots = logits_ref.shape[1]
    logits = logits_ref[...]
    top = jnp.max(logits, axis=0, keepdims=True)
    turned_ref[...] = jnp.exp(logits - top).astype(BF16).T
    tops_ref[...] = jnp.broadcast_to(top, (LANES, slots)).T
    myself = place_ref[0]
    count = 1 << len(orders[0])
    block = slots // count
    shares = path_shares(block)
    first = 0
    for path, order in enumerate(orders):
        share = shares[path]
        for place, relative in enumerate(ranks_of(order)):
            source = pl.ds(pl.multiple_of((myself ^ relative) * block + path * shares[0], 16), share)
            target = pl.ds(first + place * share, share)
            picked_ref[target, :] = turned_ref[source, :]
            picked_tops_ref[target, :] = tops_ref[source, :]
        first = first + count * share
    picked = picked_ref[...]
    sums = jnp.dot(picked, normed_ref[...], preferred_element_type=F32).astype(BF16)
    totals = jnp.dot(picked, jnp.ones((rows, LANES), BF16), preferred_element_type=F32)
    stats = pack(picked_tops_ref[...], totals)
    start = 0
    for out_ref in outs:
        end = start + out_ref.shape[0]
        out_ref[:, :width] = sums[start:end, :]
        out_ref[:, width:] = stats[start:end, :]
        start = end


def own_sums(place, normed, logits, orders):
    rows, width = normed.shape
    slots = logits.shape[1]
    count = 1 << len(orders[0])
    shares = path_shares(slots // count)
    return pl.pallas_call(
        lambda *refs: sums_kernel(orders, *refs),
        out_shape=tuple(
            jax.ShapeDtypeStruct((share * count // 2, width + LANES), BF16) for share in shares for _ in range(2)
        ),
        in_specs=[SMEM, VMEM, VMEM],
        out_specs=(VMEM,) * 4,
        scratch_shapes=[
            pltpu.VMEM((slots, rows), BF16),
            pltpu.VMEM((slots, LANES), F32),
            pltpu.VMEM((slots, rows), BF16),
            pltpu.VMEM((slots, LANES), F32),
        ],
        compiler_params=pltpu.CompilerParams(vmem_limit_bytes=24 << 20),
    )(place, normed, logits)


def merge_kernel(kept_ref, came_ref, *outs):
    width = kept_ref.shape[1] - LANES
    kept_top, kept_total = unpack(kept_ref[:, width:])
    came_top, came_total = unpack(came_ref[:, width:])
    top = jnp.maximum(kept_top, came_top)
    kept_scale, came_scale = jnp.exp(kept_top - top), jnp.exp(came_top - top)
    total = kept_total * kept_scale + came_total * came_scale
    sums = kept_ref[:, :width].astype(F32) * kept_scale + came_ref[:, :width].astype(F32) * came_scale
    if len(outs) == 1:
        outs[0][...] = (sums / total).astype(BF16)
        return
    sums = sums.astype(BF16)
    stats = pack(top, total)
    half = kept_ref.shape[0] // 2
    for index, out_ref in enumerate(outs):
        out_ref[:, :width] = sums[index * half : (index + 1) * half, :]
        out_ref[:, width:] = stats[index * half : (index + 1) * half, :]


def merge(kept, came, last):
    rows, columns = kept.shape
    if last:
        shape, specs = jax.ShapeDtypeStruct((rows, columns - LANES), BF16), VMEM
    else:
        shape, specs = (jax.ShapeDtypeStruct((rows // 2, columns), BF16),) * 2, (VMEM, VMEM)
    return pl.pallas_call(
        merge_kernel,
        out_shape=shape,
        in_specs=[VMEM, VMEM],
        out_specs=specs,
        compiler_params=pltpu.CompilerParams(vmem_limit_bytes=12 << 20),
    )(kept, came)


def experts_kernel(count, *refs):
    rows_refs, (in_a, in_b, back_a, back_b, proj_ref), refs = refs[:count], refs[count : count + 5], refs[count + 5 :]
    outs, (in_ref, back_ref, sems) = refs[:count], refs[count:]
    copies = [
        pltpu.make_async_copy(source, target, sems.at[index])
        for index, (source, target) in enumerate(((in_b, in_ref), (back_b, back_ref)))
    ]
    for copy in copies:
        copy.start()
    rows = jnp.concatenate([ref[...] for ref in rows_refs], axis=0)

    def hidden(weights):
        return jax.nn.gelu(jnp.dot(rows, weights, preferred_element_type=F32)).astype(BF16)

    total = jnp.dot(hidden(in_a[...]), back_a[...], preferred_element_type=F32)
    copies[0].wait()
    other = hidden(in_ref[...])
    copies[1].wait()
    total = total + jnp.dot(other, back_ref[...], preferred_element_type=F32)
    result = jnp.dot(total.astype(BF16), proj_ref[...], preferred_element_type=F32).astype(BF16)
    step = rows_refs[0].shape[0]
    for index, out_ref in enumerate(outs):
        out_ref[...] = result[index * step : (index + 1) * step, :]


def experts(slot_rows, first, first_other, second, second_other, w_proj):
    count = len(slot_rows)
    rows = slot_rows[0].shape[0]
    return pl.pallas_call(
        lambda *refs: experts_kernel(count, *refs),
        out_shape=(jax.ShapeDtypeStruct((rows, w_proj.shape[1]), BF16),) * count,
        in_specs=[VMEM] * count + [VMEM, HBM, VMEM, HBM, VMEM],
        out_specs=(VMEM,) * count,
        scratch_shapes=[
            pltpu.VMEM(first.shape, BF16),
            pltpu.VMEM(second.shape, BF16),
            pltpu.SemaphoreType.DMA((2,)),
        ],
        compiler_params=pltpu.CompilerParams(vmem_limit_bytes=20 << 20),
    )(*slot_rows, first, first_other, second, second_other, w_proj)


def order_kernel(ranks, starts, vis_dev, place_ref, listing_ref, filler_ref, *refs):
    pieces, out_ref, masked_ref = refs[:-2], refs[-2], refs[-1]
    total, slots = out_ref.shape
    count = len(ranks[0])
    block = total // count
    capacity = block // count
    myself = place_ref[0]
    slot = lax.broadcasted_iota(jnp.int32, (block, block), 0)
    for target in range(count):
        path, inner = divmod(target, count // 2)
        rows = [None] * count
        for relative, (index, start) in zip(ranks[path], starts[path]):
            first = start + inner * capacity
            rows[relative] = pieces[index][first : first + capacity, :]
        listing = listing_ref[:, target * block : (target + 1) * block]
        owners, order = slots_of(listing, vis_dev, count, capacity)
        visible = listing < count * vis_dev
        places = jnp.where(visible, (owners ^ myself) * capacity + order, -1)
        chosen = (places == slot).astype(F32).T.astype(BF16)
        here = pl.ds(target * block, block)
        out_ref[here, :] = jnp.dot(chosen, jnp.concatenate(rows, axis=0), preferred_element_type=F32).astype(BF16)
        shown = jnp.broadcast_to(visible.astype(F32), (LANES, block)).T[:, 0:1]
        masked_ref[here, :] = jnp.where(shown > 0.5, jnp.zeros((), F32), filler_ref[here, :].astype(F32)).astype(BF16)


def put_in_order(place, listing, filler, arrays, starts, ranks, vis_dev):
    total, width = filler.shape
    slots = arrays[0].shape[1]
    return pl.pallas_call(
        lambda *refs: order_kernel(ranks, starts, vis_dev, *refs),
        out_shape=(jax.ShapeDtypeStruct((total, slots), BF16), jax.ShapeDtypeStruct((total, width), BF16)),
        in_specs=[SMEM] + [VMEM] * (2 + len(arrays)),
        out_specs=(VMEM, VMEM),
        compiler_params=pltpu.CompilerParams(vmem_limit_bytes=20 << 20),
    )(place, listing, filler, *arrays)


def tail_kernel(
    ranks, starts, half, place_ref, combine_ref, filler_ref, w_qkv_ref, w_out_ref, *refs
):
    pieces = refs[:-5]
    out_ref, slot_ref, k_ref, v_ref, a_ref = refs[-5:]
    mine, width = out_ref.shape
    total = combine_ref.shape[0]
    head_dim = width // HEADS
    groups = width // LANES
    in_group = LANES // head_dim
    myself = place_ref[0]
    for path in range(2):
        for relative, (index, start) in zip(ranks[path], starts[path]):
            target = pl.multiple_of((myself ^ relative) * (2 * half) + path * half, half)
            slot_ref[pl.ds(target, half), :] = pieces[index][start : start + half, :]
    slot_rows = slot_ref[...]
    w_kv = w_qkv_ref[:, width:]

    def positions(block, many=1):
        rows = pl.ds(block * mine * many, mine * many) if isinstance(block, int) else pl.ds(pl.multiple_of(block * mine, mine), mine)
        shown = jnp.dot(combine_ref[rows, :], slot_rows, preferred_element_type=F32).astype(BF16)
        dec_in = shown.astype(F32) + filler_ref[rows, :].astype(F32)
        return rows, dec_in, normalise(dec_in).astype(BF16)

    v_ref[:, :, LANES:] = jnp.ones((groups, total, LANES), BF16)
    for block in range(total // mine // 8):
        rows, _, normed = positions(block, 8)
        kv = jnp.dot(normed, w_kv, preferred_element_type=F32).astype(BF16)
        for group in range(groups):
            k_ref[group, rows, :] = kv[:, group * LANES : (group + 1) * LANES]
            v_ref[group, rows, :LANES] = kv[:, width + group * LANES : width + (group + 1) * LANES]

    _, dec_in, normed = positions(myself)
    queries = jnp.dot(normed, w_qkv_ref[:, :width], preferred_element_type=F32).astype(BF16)
    head_of = lax.broadcasted_iota(jnp.int32, (mine, LANES), 1) // head_dim
    factor = math.log2(math.e) / math.sqrt(head_dim)

    for group in range(groups):
        q_group = queries[:, group * LANES : (group + 1) * LANES]
        result = jnp.zeros((mine, LANES), F32)
        for head in range(in_group):
            q_head = jnp.where(head_of == head, q_group, jnp.zeros_like(q_group))
            scores = lax.dot_general(
                q_head, k_ref[group], (((1,), (1,)), ((), ())), preferred_element_type=F32
            )
            highest = jnp.max(scores, axis=1, keepdims=True)
            raised = jnp.exp2((scores - highest) * factor).astype(BF16)
            both = jnp.dot(raised, v_ref[group], preferred_element_type=F32)
            result = jnp.where(head_of == head, both[:, :LANES] / both[:, LANES:], result)
        a_ref[group] = result.astype(BF16)

    attended = jnp.concatenate([a_ref[group] for group in range(groups)], axis=1)
    mixed = jnp.dot(attended, w_out_ref[...], preferred_element_type=F32)
    out_ref[...] = (mixed + dec_in).astype(BF16)


def tail(place, combine, filler, w_qkv, w_out, arrays, starts, ranks, half):
    total, width = filler.shape
    groups = width // LANES
    mine = total // len(ranks[0])
    return pl.pallas_call(
        lambda *refs: tail_kernel(ranks, starts, half, *refs),
        out_shape=jax.ShapeDtypeStruct((mine, width), BF16),
        in_specs=[SMEM] + [VMEM] * (4 + len(arrays)),
        out_specs=VMEM,
        scratch_shapes=[
            pltpu.VMEM((combine.shape[1], width), BF16),
            pltpu.VMEM((groups, total, LANES), BF16),
            pltpu.VMEM((groups, total, 2 * LANES), BF16),
            pltpu.VMEM((groups, mine, LANES), BF16),
        ],
        compiler_params=pltpu.CompilerParams(vmem_limit_bytes=32 << 20),
    )(place, combine, filler, w_qkv, w_out, *arrays)


def sinusoid_table(count, block, width):
    half = width // 2
    speeds = jnp.exp(-math.log(10000.0) * jnp.arange(half).astype(F32) / half)
    far = (jnp.arange(count // block) * block).astype(F32)[:, None] * speeds[None, :]
    near = jnp.arange(block).astype(F32)[:, None] * speeds[None, :]
    far_sin, far_cos = jnp.sin(far)[:, None, :], jnp.cos(far)[:, None, :]
    near_sin, near_cos = jnp.sin(near)[None], jnp.cos(near)[None]
    sines = far_sin * near_cos + far_cos * near_sin
    cosines = far_cos * near_cos - far_sin * near_sin
    return jnp.concatenate([sines, cosines], axis=2).reshape(count, width)


def per_device(tokens, slot_keys, w_in, w_back, w_proj, dec_source, mask_token, w_qkv, w_out):
    vis_dev, width = tokens.shape
    n_tok = lax.axis_size("tok")
    n_clip = lax.axis_size("clip")
    slots = slot_keys.shape[1]
    dec_width = w_proj.shape[1]
    dec_total = dec_source.shape[1]
    dec_dev = dec_total // n_tok
    myself = lax.axis_index("tok").astype(jnp.int32)
    place = myself.reshape(1)
    orders = bit_orders(n_tok)
    back_orders = tuple(order[::-1] for order in orders)
    ranks = tuple(gathered_ranks(order) for order in back_orders)
    steps = len(orders[0])

    first, first_other = w_in[0], swap(w_in[0], "clip", 1)
    second, second_other = w_back[0], swap(w_back[0], "clip", 1)

    outgoing, normed, logits = rows_and_picks(place, dec_source, tokens, slot_keys, n_tok)
    arrays, starts, brought = gather_pair(outgoing, "tok", back_orders)
    filler = (mask_token.astype(F32)[None, :] + sinusoid_table(dec_total, dec_dev, dec_width)).astype(BF16)
    ordered, filler = put_in_order(place, dec_source, filler, arrays, starts, ranks, vis_dev)

    quarters = own_sums(place, normed, logits, orders)
    state = [(quarters[0], quarters[1]), (quarters[2], quarters[3])]
    for step in range(steps):
        sent = [state[path][1] for path in range(2)]
        arrived = [swap(sent[path], "tok", 1 << orders[path][step]) for path in range(2)]
        state = [merge(state[path][0], arrived[path], step == steps - 1) for path in range(2)]
    slot_in = jnp.concatenate(state, axis=0)

    others = [2 * step for step in range(1, n_clip // 2)]
    rows = [slot_in] + [swap(slot_in, "clip", mask) for mask in others]
    rows = list(tie(rows, [array for group in brought[1:-1] for array in group]))
    results = experts(rows, first, first_other, second, second_other, w_proj)
    slot_proj = results[0].astype(F32)
    for mask, result in zip(others, results[1:]):
        slot_proj = slot_proj + swap(result, "clip", mask).astype(F32)
    (slot_proj,) = tie([slot_proj.astype(BF16)], brought[-1])
    everyone, their_starts, their_ranks = gather_direct(slot_proj, "tok")
    return tail(place, ordered, filler, w_qkv, w_out, everyone, their_starts, their_ranks, slot_proj.shape[0] // 2)


def solution(mesh):
    placed = (
        P(("clip", "tok"), None),
        P(),
        P("tok", None, "clip"),
        P("tok", "clip", None),
        P(),
        P("clip", None),
        P(),
        P(),
        P(),
    )
    return jax.shard_map(
        per_device, mesh=mesh, in_specs=placed, out_specs=P(("clip", "tok"), None), check_vma=False
    )
```

```python
import math

import jax
import jax.numpy as jnp
from jax import lax
from jax.experimental import pallas as pl
from jax.experimental.pallas import tpu as pltpu
from jax.sharding import PartitionSpec as P

HEADS = 16
LANES = 128
F32 = jnp.float32
BF16 = jnp.bfloat16
VMEM = pl.BlockSpec(memory_space=pltpu.VMEM)
SMEM = pl.BlockSpec(memory_space=pltpu.SMEM)
HBM = pl.BlockSpec(memory_space=pltpu.HBM)


def normalise(values):
    centre = values - jnp.mean(values, axis=-1, keepdims=True)
    spread = jnp.mean(centre * centre, axis=-1, keepdims=True)
    return centre * lax.rsqrt(spread + 1e-05)


def thirds(column):
    high = column.astype(BF16)
    rest = column - high.astype(F32)
    middle = rest.astype(BF16)
    low = (rest - middle.astype(F32)).astype(BF16)
    return high, middle, low


def pack(tops, totals):
    rows = max(tops.shape[0], totals.shape[0])
    lane = lax.broadcasted_iota(jnp.int32, (rows, LANES), 1)
    packed = jnp.zeros((rows, LANES), F32)
    for place, piece in enumerate(thirds(tops) + thirds(totals)):
        packed = jnp.where(lane == place, piece.astype(F32), packed)
    return packed.astype(BF16)


def unpack(stats):
    parts = stats.astype(F32)
    top = parts[:, 0:1] + parts[:, 1:2] + parts[:, 2:3]
    total = parts[:, 3:4] + parts[:, 4:5] + parts[:, 5:6]
    return top, total


def swap(values, axis, mask):
    count = lax.axis_size(axis)
    return lax.ppermute(values, axis, [(index, index ^ mask) for index in range(count)])


def bit_orders(count):
    bits = list(range(count.bit_length() - 1))
    first = bits[1:2] + bits[0:1] + bits[2:]
    second = bits
    return first, second


def path_shares(block):
    return (block // 4, block - block // 4) if block % 64 == 0 else (block // 2, block // 2)


def ranks_of(order):
    steps = len(order)
    return [
        sum(((place >> (steps - 1 - step)) & 1) << bit for step, bit in enumerate(order))
        for place in range(1 << steps)
    ]


def gather_pair(values, axis, orders):
    rows = values.shape[0]
    half = rows // 2
    arrays, steps = [values], []
    starts = [[(0, 0)], [(0, half)]]
    for step, (first, second) in enumerate(zip(*orders)):
        together = orders[0][: step + 1] == orders[1][: step + 1]
        if together:
            held = arrays[0] if len(arrays) == 1 else jnp.concatenate(arrays, axis=0)
            count = held.shape[0] // rows
            arrays.append(swap(held, axis, 1 << first))
            for path in range(2):
                starts[path] = starts[path] + [(len(arrays) - 1, index * rows + path * half) for index in range(count)]
            steps.append([arrays[-1]])
            continue
        fresh = []
        for path, bit in enumerate((first, second)):
            held = jnp.concatenate([arrays[index][row : row + half] for index, row in starts[path]], axis=0)
            fresh.append(swap(held, axis, 1 << bit))
        for path in range(2):
            index = len(arrays) + path
            starts[path] = starts[path] + [(index, place * half) for place in range(len(starts[path]))]
        arrays = arrays + fresh
        steps.append(fresh)
    return arrays, starts, steps


def gather_direct(values, axis):
    count = lax.axis_size(axis)
    bits = count.bit_length() - 1
    low = 1 << (bits // 2)
    rows = values.shape[0]
    near = [values] + [swap(values, axis, step) for step in range(1, low)]
    held = jnp.concatenate(near, axis=0)
    arrays = [held] + [swap(held, axis, step * low) for step in range(1, count // low)]
    ranks = [step * low + inner for step in range(count // low) for inner in range(low)]
    starts = [
        [(step, inner * rows + half) for step in range(count // low) for inner in range(low)] for half in (0, rows // 2)
    ]
    return arrays, starts, (ranks, ranks)


def tie(values, others):
    kept = lax.optimization_barrier((tuple(values), tuple(others)))
    return kept[0]


def gathered_ranks(order):
    held = [0]
    for bit in order:
        held = held + [index ^ (1 << bit) for index in held]
    return held


def slots_of(listing, vis_dev, count, capacity):
    block = listing.shape[1]
    owners = listing // vis_dev
    across = jnp.broadcast_to(owners, (block, block))
    before = lax.broadcasted_iota(jnp.int32, (block, block), 0) < lax.broadcasted_iota(jnp.int32, (block, block), 1)
    same = (across == across.T) & before
    ranks = jnp.sum(same.astype(F32), axis=0, keepdims=True).astype(jnp.int32)
    return owners, jnp.minimum(ranks, capacity - 1)


def picker_of(myself, listing_ref, vis_dev, count):
    block = listing_ref.shape[1] // count
    capacity = block // count
    row = lax.broadcasted_iota(jnp.int32, (capacity, block), 0)
    token = lax.broadcasted_iota(jnp.int32, (capacity, vis_dev), 1)
    picks = []
    for target in range(count):
        listing = listing_ref[:, target * block : (target + 1) * block]
        owners, ranks = slots_of(listing, vis_dev, count, capacity)
        mine = jnp.where(owners == myself, ranks, -1)
        local = jnp.broadcast_to(listing - myself * vis_dev + 1, (capacity, block))
        source = jnp.sum(jnp.where(mine == row, local, 0).astype(F32), axis=1, keepdims=True).astype(jnp.int32) - 1
        picks.append((source == token).astype(BF16))
    return jnp.concatenate(picks, axis=0)


def rows_kernel(count, place_ref, listing_hbm, tokens_hbm, keys_hbm, picked_ref, normed_ref, logits_ref, *refs):
    listing_ref, tokens_ref, keys_ref, listing_sem, sems = refs
    listing_copy = pltpu.make_async_copy(listing_hbm, listing_ref, listing_sem)
    listing_copy.start()
    rows, width = tokens_ref.shape
    pieces = sems.shape[1]
    token_step, key_step = rows // pieces, width // pieces
    copies = []
    for piece in range(pieces):
        part = pl.ds(piece * token_step, token_step)
        copies.append(pltpu.make_async_copy(tokens_hbm.at[part], tokens_ref.at[part], sems.at[0, piece]))
    for piece in range(pieces):
        part = pl.ds(piece * key_step, key_step)
        copies.append(pltpu.make_async_copy(keys_hbm.at[part], keys_ref.at[part], sems.at[1, piece]))
    for copy in copies:
        copy.start()
    listing_copy.wait()
    picker = picker_of(place_ref[0], listing_ref, rows, count)
    parts = []
    for piece in range(pieces):
        copies[piece].wait()
        part = tokens_ref[piece * token_step : (piece + 1) * token_step, :].astype(F32)
        parts.append(normalise(part).astype(BF16))
    normed = jnp.concatenate(parts, axis=0)
    normed_ref[...] = normed
    for copy in copies[pieces:]:
        copy.wait()
    logits = jnp.dot(normed, keys_ref[...], preferred_element_type=F32)
    logits_ref[...] = logits
    raised = jnp.exp(logits - jnp.max(logits, axis=1, keepdims=True))
    combine = (raised / jnp.sum(raised, axis=1, keepdims=True)).astype(BF16)
    picked_ref[...] = jnp.dot(picker, combine, preferred_element_type=F32).astype(BF16)


def rows_and_picks(place, listing, tokens, slot_keys, count):
    rows, width = tokens.shape
    slots = slot_keys.shape[1]
    pieces = 4
    return pl.pallas_call(
        lambda *refs: rows_kernel(count, *refs),
        out_shape=(
            jax.ShapeDtypeStruct((listing.shape[1] // count, slots), BF16),
            jax.ShapeDtypeStruct((rows, width), BF16),
            jax.ShapeDtypeStruct((rows, slots), F32),
        ),
        in_specs=[SMEM, HBM, HBM, HBM],
        out_specs=(VMEM,) * 3,
        scratch_shapes=[
            pltpu.VMEM(listing.shape, jnp.int32),
            pltpu.VMEM((rows, width), BF16),
            pltpu.VMEM((width, slots), BF16),
            pltpu.SemaphoreType.DMA,
            pltpu.SemaphoreType.DMA((2, pieces)),
        ],
        compiler_params=pltpu.CompilerParams(vmem_limit_bytes=24 << 20),
    )(place, *(pltpu.with_memory_space_constraint(array, pltpu.HBM) for array in (listing, tokens, slot_keys)))


def sums_kernel(orders, place_ref, normed_ref, logits_ref, *refs):
    outs, (turned_ref, tops_ref, picked_ref, picked_tops_ref) = refs[:4], refs[4:]
    rows, width = normed_ref.shape
    slots = logits_ref.shape[1]
    logits = logits_ref[...]
    top = jnp.max(logits, axis=0, keepdims=True)
    turned_ref[...] = jnp.exp(logits - top).astype(BF16).T
    tops_ref[...] = jnp.broadcast_to(top, (LANES, slots)).T
    myself = place_ref[0]
    count = 1 << len(orders[0])
    block = slots // count
    shares = path_shares(block)
    first = 0
    for path, order in enumerate(orders):
        share = shares[path]
        for place, relative in enumerate(ranks_of(order)):
            source = pl.ds(pl.multiple_of((myself ^ relative) * block + path * shares[0], 16), share)
            target = pl.ds(first + place * share, share)
            picked_ref[target, :] = turned_ref[source, :]
            picked_tops_ref[target, :] = tops_ref[source, :]
        first = first + count * share
    picked = picked_ref[...]
    sums = jnp.dot(picked, normed_ref[...], preferred_element_type=F32).astype(BF16)
    totals = jnp.dot(picked, jnp.ones((rows, LANES), BF16), preferred_element_type=F32)
    stats = pack(picked_tops_ref[...], totals)
    start = 0
    for out_ref in outs:
        end = start + out_ref.shape[0]
        out_ref[:, :width] = sums[start:end, :]
        out_ref[:, width:] = stats[start:end, :]
        start = end


def own_sums(place, normed, logits, orders):
    rows, width = normed.shape
    slots = logits.shape[1]
    count = 1 << len(orders[0])
    shares = path_shares(slots // count)
    return pl.pallas_call(
        lambda *refs: sums_kernel(orders, *refs),
        out_shape=tuple(
            jax.ShapeDtypeStruct((share * count // 2, width + LANES), BF16) for share in shares for _ in range(2)
        ),
        in_specs=[SMEM, VMEM, VMEM],
        out_specs=(VMEM,) * 4,
        scratch_shapes=[
            pltpu.VMEM((slots, rows), BF16),
            pltpu.VMEM((slots, LANES), F32),
            pltpu.VMEM((slots, rows), BF16),
            pltpu.VMEM((slots, LANES), F32),
        ],
        compiler_params=pltpu.CompilerParams(vmem_limit_bytes=24 << 20),
    )(place, normed, logits)


def merge_kernel(kept_ref, came_ref, *outs):
    width = kept_ref.shape[1] - LANES
    kept_top, kept_total = unpack(kept_ref[:, width:])
    came_top, came_total = unpack(came_ref[:, width:])
    top = jnp.maximum(kept_top, came_top)
    kept_scale, came_scale = jnp.exp(kept_top - top), jnp.exp(came_top - top)
    total = kept_total * kept_scale + came_total * came_scale
    sums = kept_ref[:, :width].astype(F32) * kept_scale + came_ref[:, :width].astype(F32) * came_scale
    if len(outs) == 1:
        outs[0][...] = (sums / total).astype(BF16)
        return
    sums = sums.astype(BF16)
    stats = pack(top, total)
    half = kept_ref.shape[0] // 2
    for index, out_ref in enumerate(outs):
        out_ref[:, :width] = sums[index * half : (index + 1) * half, :]
        out_ref[:, width:] = stats[index * half : (index + 1) * half, :]


def merge(kept, came, last):
    rows, columns = kept.shape
    if last:
        shape, specs = jax.ShapeDtypeStruct((rows, columns - LANES), BF16), VMEM
    else:
        shape, specs = (jax.ShapeDtypeStruct((rows // 2, columns), BF16),) * 2, (VMEM, VMEM)
    return pl.pallas_call(
        merge_kernel,
        out_shape=shape,
        in_specs=[VMEM, VMEM],
        out_specs=specs,
        compiler_params=pltpu.CompilerParams(vmem_limit_bytes=12 << 20),
    )(kept, came)


def experts_kernel(count, *refs):
    rows_refs, (in_a, in_b, back_a, back_b, proj_ref), refs = refs[:count], refs[count : count + 5], refs[count + 5 :]
    outs, (in_ref, back_ref, sems) = refs[:count], refs[count:]
    copies = [
        pltpu.make_async_copy(source, target, sems.at[index])
        for index, (source, target) in enumerate(((in_b, in_ref), (back_b, back_ref)))
    ]
    for copy in copies:
        copy.start()
    rows = jnp.concatenate([ref[...] for ref in rows_refs], axis=0)

    def hidden(weights):
        return jax.nn.gelu(jnp.dot(rows, weights, preferred_element_type=F32)).astype(BF16)

    total = jnp.dot(hidden(in_a[...]), back_a[...], preferred_element_type=F32)
    copies[0].wait()
    other = hidden(in_ref[...])
    copies[1].wait()
    total = total + jnp.dot(other, back_ref[...], preferred_element_type=F32)
    result = jnp.dot(total.astype(BF16), proj_ref[...], preferred_element_type=F32).astype(BF16)
    step = rows_refs[0].shape[0]
    for index, out_ref in enumerate(outs):
        out_ref[...] = result[index * step : (index + 1) * step, :]


def experts(slot_rows, first, first_other, second, second_other, w_proj):
    count = len(slot_rows)
    rows = slot_rows[0].shape[0]
    return pl.pallas_call(
        lambda *refs: experts_kernel(count, *refs),
        out_shape=(jax.ShapeDtypeStruct((rows, w_proj.shape[1]), BF16),) * count,
        in_specs=[VMEM] * count + [VMEM, HBM, VMEM, HBM, VMEM],
        out_specs=(VMEM,) * count,
        scratch_shapes=[
            pltpu.VMEM(first.shape, BF16),
            pltpu.VMEM(second.shape, BF16),
            pltpu.SemaphoreType.DMA((2,)),
        ],
        compiler_params=pltpu.CompilerParams(vmem_limit_bytes=20 << 20),
    )(*slot_rows, first, first_other, second, second_other, w_proj)


def order_kernel(ranks, starts, vis_dev, place_ref, listing_ref, filler_ref, *refs):
    pieces, out_ref, masked_ref = refs[:-2], refs[-2], refs[-1]
    total, slots = out_ref.shape
    count = len(ranks[0])
    block = total // count
    capacity = block // count
    myself = place_ref[0]
    slot = lax.broadcasted_iota(jnp.int32, (block, block), 0)
    for target in range(count):
        path, inner = divmod(target, count // 2)
        rows = [None] * count
        for relative, (index, start) in zip(ranks[path], starts[path]):
            first = start + inner * capacity
            rows[relative] = pieces[index][first : first + capacity, :]
        listing = listing_ref[:, target * block : (target + 1) * block]
        owners, order = slots_of(listing, vis_dev, count, capacity)
        visible = listing < count * vis_dev
        places = jnp.where(visible, (owners ^ myself) * capacity + order, -1)
        chosen = (places == slot).astype(F32).T.astype(BF16)
        here = pl.ds(target * block, block)
        out_ref[here, :] = jnp.dot(chosen, jnp.concatenate(rows, axis=0), preferred_element_type=F32).astype(BF16)
        shown = jnp.broadcast_to(visible.astype(F32), (LANES, block)).T[:, 0:1]
        masked_ref[here, :] = jnp.where(shown > 0.5, jnp.zeros((), F32), filler_ref[here, :].astype(F32)).astype(BF16)


def put_in_order(place, listing, filler, arrays, starts, ranks, vis_dev):
    total, width = filler.shape
    slots = arrays[0].shape[1]
    return pl.pallas_call(
        lambda *refs: order_kernel(ranks, starts, vis_dev, *refs),
        out_shape=(jax.ShapeDtypeStruct((total, slots), BF16), jax.ShapeDtypeStruct((total, width), BF16)),
        in_specs=[SMEM] + [VMEM] * (2 + len(arrays)),
        out_specs=(VMEM, VMEM),
        compiler_params=pltpu.CompilerParams(vmem_limit_bytes=20 << 20),
    )(place, listing, filler, *arrays)


def tail_kernel(
    ranks, starts, half, place_ref, combine_ref, filler_ref, w_qkv_ref, w_out_ref, *refs
):
    pieces = refs[:-5]
    out_ref, slot_ref, k_ref, v_ref, a_ref = refs[-5:]
    mine, width = out_ref.shape
    total = combine_ref.shape[0]
    head_dim = width // HEADS
    groups = width // LANES
    in_group = LANES // head_dim
    myself = place_ref[0]
    for path in range(2):
        for relative, (index, start) in zip(ranks[path], starts[path]):
            target = pl.multiple_of((myself ^ relative) * (2 * half) + path * half, half)
            slot_ref[pl.ds(target, half), :] = pieces[index][start : start + half, :]
    slot_rows = slot_ref[...]
    w_kv = w_qkv_ref[:, width:]

    def positions(block, many=1):
        rows = pl.ds(block * mine * many, mine * many) if isinstance(block, int) else pl.ds(pl.multiple_of(block * mine, mine), mine)
        shown = jnp.dot(combine_ref[rows, :], slot_rows, preferred_element_type=F32).astype(BF16)
        dec_in = shown.astype(F32) + filler_ref[rows, :].astype(F32)
        return rows, dec_in, normalise(dec_in).astype(BF16)

    v_ref[:, :, LANES:] = jnp.ones((groups, total, LANES), BF16)
    for block in range(total // mine // 8):
        rows, _, normed = positions(block, 8)
        kv = jnp.dot(normed, w_kv, preferred_element_type=F32).astype(BF16)
        for group in range(groups):
            k_ref[group, rows, :] = kv[:, group * LANES : (group + 1) * LANES]
            v_ref[group, rows, :LANES] = kv[:, width + group * LANES : width + (group + 1) * LANES]

    _, dec_in, normed = positions(myself)
    queries = jnp.dot(normed, w_qkv_ref[:, :width], preferred_element_type=F32).astype(BF16)
    head_of = lax.broadcasted_iota(jnp.int32, (mine, LANES), 1) // head_dim
    factor = math.log2(math.e) / math.sqrt(head_dim)

    for group in range(groups):
        q_group = queries[:, group * LANES : (group + 1) * LANES]
        result = jnp.zeros((mine, LANES), F32)
        for head in range(in_group):
            q_head = jnp.where(head_of == head, q_group, jnp.zeros_like(q_group))
            scores = lax.dot_general(
                q_head, k_ref[group], (((1,), (1,)), ((), ())), preferred_element_type=F32
            )
            highest = jnp.max(scores, axis=1, keepdims=True)
            raised = jnp.exp2((scores - highest) * factor).astype(BF16)
            both = jnp.dot(raised, v_ref[group], preferred_element_type=F32)
            result = jnp.where(head_of == head, both[:, :LANES] / both[:, LANES:], result)
        a_ref[group] = result.astype(BF16)

    attended = jnp.concatenate([a_ref[group] for group in range(groups)], axis=1)
    mixed = jnp.dot(attended, w_out_ref[...], preferred_element_type=F32)
    out_ref[...] = (mixed + dec_in).astype(BF16)


def tail(place, combine, filler, w_qkv, w_out, arrays, starts, ranks, half):
    total, width = filler.shape
    groups = width // LANES
    mine = total // len(ranks[0])
    return pl.pallas_call(
        lambda *refs: tail_kernel(ranks, starts, half, *refs),
        out_shape=jax.ShapeDtypeStruct((mine, width), BF16),
        in_specs=[SMEM] + [VMEM] * (4 + len(arrays)),
        out_specs=VMEM,
        scratch_shapes=[
            pltpu.VMEM((combine.shape[1], width), BF16),
            pltpu.VMEM((groups, total, LANES), BF16),
            pltpu.VMEM((groups, total, 2 * LANES), BF16),
            pltpu.VMEM((groups, mine, LANES), BF16),
        ],
        compiler_params=pltpu.CompilerParams(vmem_limit_bytes=32 << 20),
    )(place, combine, filler, w_qkv, w_out, *arrays)


def sinusoid_table(count, block, width):
    half = width // 2
    speeds = jnp.exp(-math.log(10000.0) * jnp.arange(half).astype(F32) / half)
    far = (jnp.arange(count // block) * block).astype(F32)[:, None] * speeds[None, :]
    near = jnp.arange(block).astype(F32)[:, None] * speeds[None, :]
    far_sin, far_cos = jnp.sin(far)[:, None, :], jnp.cos(far)[:, None, :]
    near_sin, near_cos = jnp.sin(near)[None], jnp.cos(near)[None]
    sines = far_sin * near_cos + far_cos * near_sin
    cosines = far_cos * near_cos - far_sin * near_sin
    return jnp.concatenate([sines, cosines], axis=2).reshape(count, width)


def per_device(tokens, slot_keys, w_in, w_back, w_proj, dec_source, mask_token, w_qkv, w_out):
    vis_dev, width = tokens.shape
    n_tok = lax.axis_size("tok")
    n_clip = lax.axis_size("clip")
    slots = slot_keys.shape[1]
    dec_width = w_proj.shape[1]
    dec_total = dec_source.shape[1]
    dec_dev = dec_total // n_tok
    myself = lax.axis_index("tok").astype(jnp.int32)
    place = myself.reshape(1)
    orders = bit_orders(n_tok)
    back_orders = tuple(order[::-1] for order in orders)
    ranks = tuple(gathered_ranks(order) for order in back_orders)
    steps = len(orders[0])

    first, first_other = w_in[0], swap(w_in[0], "clip", 1)
    second, second_other = w_back[0], swap(w_back[0], "clip", 1)

    outgoing, normed, logits = rows_and_picks(place, dec_source, tokens, slot_keys, n_tok)
    arrays, starts, brought = gather_pair(outgoing, "tok", back_orders)
    filler = (mask_token.astype(F32)[None, :] + sinusoid_table(dec_total, dec_dev, dec_width)).astype(BF16)
    ordered, filler = put_in_order(place, dec_source, filler, arrays, starts, ranks, vis_dev)

    quarters = own_sums(place, normed, logits, orders)
    state = [(quarters[0], quarters[1]), (quarters[2], quarters[3])]
    for step in range(steps):
        sent = [state[path][1] for path in range(2)]
        arrived = [swap(sent[path], "tok", 1 << orders[path][step]) for path in range(2)]
        state = [merge(state[path][0], arrived[path], step == steps - 1) for path in range(2)]
    slot_in = jnp.concatenate(state, axis=0)

    others = [2 * step for step in range(1, n_clip // 2)]
    rows = [slot_in] + [swap(slot_in, "clip", mask) for mask in others]
    results = experts(rows, first, first_other, second, second_other, w_proj)
    slot_proj = results[0].astype(F32)
    for mask, result in zip(others, results[1:]):
        slot_proj = slot_proj + swap(result, "clip", mask).astype(F32)
    (slot_proj,) = tie([slot_proj.astype(BF16)], brought[-1])
    everyone, their_starts, their_ranks = gather_direct(slot_proj, "tok")
    return tail(place, ordered, filler, w_qkv, w_out, everyone, their_starts, their_ranks, slot_proj.shape[0] // 2)


def solution(mesh):
    placed = (
        P(("clip", "tok"), None),
        P(),
        P("tok", None, "clip"),
        P("tok", "clip", None),
        P(),
        P("clip", None),
        P(),
        P(),
        P(),
    )
    return jax.shard_map(
        per_device, mesh=mesh, in_specs=placed, out_specs=P(("clip", "tok"), None), check_vma=False
    )
```
